512 devices in a mesh: tm: 16 (over z), height: 32 (over x, y, core).
Axes of the slice: x: 4, y: 4, z: 16, core: 2. Of those that a mesh axis runs over, the one named last changes fastest.
Arguments:
- latent: bfloat16 [32, 64, 16, 256], P('tm', 'height'), may hold values from -6 to 6
- target_frames: bfloat16 [32, 128, 32, 128], P('tm', 'height'), may hold values from -6 to 6
- master: float32 [256, 3456], P('height'), may hold values from -1.5 to 1.5
- first_moment: float32 [256, 3456], P('height'), may hold values from -18 to 18
- second_moment: float32 [256, 3456], P('height'), may hold values from 1 to 10
- ema_weights: float32 [256, 3456], P('height'), may hold values from -6 to 6
Outputs:
- new_master: float32 [256, 3456], P('height')
- new_first: float32 [256, 3456], P('height')
- new_second: float32 [256, 3456], P('height')
- new_ema: float32 [256, 3456], P('height')
- latent_grad: bfloat16 [32, 64, 16, 256], P('tm', 'height')
- recon_loss: float32 [], replicated
The draws below stay inside these ranges and needn't reach their ends.
All inputs are finite; a program needn't handle non-finite values.
Results may differ from the reference program's by a relative error of at most 0.0056.
Values may be sent and summed in bfloat16 or wider, within the bound.
A program may use at most 64 MiB of HBM per device.

```python
import math
import jax
import jax.numpy as jnp
from jax import lax

C = 256
O = 128
WL = 16
FRAMES = 32
LROWS = 64
TAPS = 3456


def steps_of(stream_key, shape, cuts, least, high):
    def one(axis_at, shards_of):
        heights = jax.random.uniform(jax.random.fold_in(jax.random.fold_in(stream_key, 6), axis_at), (shards_of,), jnp.float32, least / len(cuts), high / len(cuts))
        return jnp.repeat(jnp.exp(heights), shape[axis_at] // shards_of).reshape((-1,) + (1,) * (len(shape) - axis_at - 1))

    gain = one(*cuts[0])
    for cut in cuts[1:]:
        gain = gain * one(*cut)
    return gain


def scatter_about(own_key, shape, deviation, reach, shards=(), dtype=jnp.bfloat16):
    loudness = steps_of(own_key, shape, shards, -0.22, 0.18) if shards else 1.0
    values = jax.random.normal(own_key, shape, jnp.float32) * deviation * loudness
    return jnp.minimum(jnp.maximum(values, -reach), reach).astype(dtype)


def setup_inputs(seed: int = 0) -> dict:
    key_of = jax.random.split(jax.random.key(seed), 7)
    latent = scatter_about(key_of[0], (FRAMES, LROWS, WL, C), 1.0, 6.0, ((0, 16), (1, 32)))
    target_frames = scatter_about(key_of[1], (FRAMES, 2 * LROWS, 2 * WL, O), 1.0, 6.0, ((0, 16), (1, 32)))
    master = scatter_about(key_of[2], (C, TAPS), 0.25, 1.5, ((0, 32),), jnp.float32)
    first_moment = scatter_about(key_of[3], (C, TAPS), 3.0, 18.0, ((0, 32),), jnp.float32)
    second_moment = jnp.clip(jnp.exp(math.log(10.0) - 2.3025851 * jax.random.uniform(key_of[4], (C, TAPS), jnp.float32) ** steps_of(key_of[4], (C, TAPS), ((0, 32),), -0.2, 0.2)), 1.0, 10.0)
    ema_weights = scatter_about(key_of[5], (C, TAPS), 1.0, 6.0, ((0, 32),), jnp.float32)
    return dict(latent=latent, target_frames=target_frames, master=master, first_moment=first_moment, second_moment=second_moment, ema_weights=ema_weights)


learn_rate = 0.3
beta_first = 0.9
beta_second = 0.99
ema_decay = 0.9
adam_eps = 1e-08

def tap_offsets():
    return [(tap_time, tap_row, tap_col) for tap_time in range(3) for tap_row in range(3) for tap_col in range(3)]

def reference(latent, target_frames, master, first_moment, second_moment, ema_weights):
    frames, low_rows, low_cols, channels = latent.shape
    outputs = target_frames.shape[3]
    rows = 2 * low_rows
    cols = 2 * low_cols
    cells = frames * rows * cols
    scale = 1.0 / math.sqrt(27 * channels)
    kernel = (master * scale).astype(jnp.bfloat16)
    upsampled = jnp.repeat(jnp.repeat(latent, 2, axis=1), 2, axis=2)
    padded = jnp.pad(upsampled, ((2, 0), (1, 1), (1, 1), (0, 0)))
    result = jnp.zeros((cells, outputs), jnp.float32)
    for index, (tap_time, tap_row, tap_col) in enumerate(tap_offsets()):
        window = padded[tap_time:tap_time + frames, tap_row:tap_row + rows, tap_col:tap_col + cols].reshape(cells, channels)
        result = result + jnp.dot(window, kernel[:, index * outputs:(index + 1) * outputs], preferred_element_type=jnp.float32)
    misfit = result - target_frames.reshape(cells, outputs).astype(jnp.float32)
    recon_loss = jnp.sum(misfit * misfit) / (cells * outputs)
    out_grad = misfit.astype(jnp.bfloat16)
    grad_padded = jnp.pad(out_grad.reshape(frames, rows, cols, outputs), ((0, 2), (1, 1), (1, 1), (0, 0)))
    spread = jnp.zeros((cells, channels), jnp.float32)
    pieces = []
    for index, (tap_time, tap_row, tap_col) in enumerate(tap_offsets()):
        column = kernel[:, index * outputs:(index + 1) * outputs]
        window = grad_padded[2 - tap_time:2 - tap_time + frames, 2 - tap_row:2 - tap_row + rows, 2 - tap_col:2 - tap_col + cols].reshape(cells, outputs)
        spread = spread + lax.dot_general(window, column, (((1,), (1,)), ((), ())), preferred_element_type=jnp.float32)
        source = padded[tap_time:tap_time + frames, tap_row:tap_row + rows, tap_col:tap_col + cols].reshape(cells, channels)
        pieces.append(lax.dot_general(source, out_grad, (((0,), (0,)), ((), ())), preferred_element_type=jnp.float32))
    latent_grad = spread.reshape(frames, low_rows, 2, low_cols, 2, channels).sum(axis=(2, 4)).astype(jnp.bfloat16)
    kernel_grad = scale * jnp.concatenate(pieces, axis=1)
    new_first = beta_first * first_moment + (1.0 - beta_first) * kernel_grad
    new_second = beta_second * second_moment + (1.0 - beta_second) * kernel_grad * kernel_grad
    new_master = master - learn_rate * new_first / (jnp.sqrt(new_second) + adam_eps)
    new_ema = ema_decay * ema_weights + (1.0 - ema_decay) * new_master
    return (new_master, new_first, new_second, new_ema, latent_grad, recon_loss)
```

```python
import math

import jax
import jax.numpy as jnp
from jax import lax
from jax.experimental import pallas as pl
from jax.experimental.pallas import tpu as pltpu
from jax.sharding import PartitionSpec as P

learn_rate = 0.3
beta_first = 0.9
beta_second = 0.99
ema_decay = 0.9
adam_eps = 1e-08

MESH = pl.DeviceIdType.MESH
F32 = jnp.float32
BF16 = jnp.bfloat16
SCALE = 1.0 / math.sqrt(27 * 256)
WIDE = 640
CUT = 384
PARTS = ((0, CUT), (CUT, WIDE - CUT))
Z = 16


def low_lanes(shape):
    return lax.broadcasted_iota(jnp.int32, shape, len(shape) - 1) < 64


def swap_lanes(v):
    return pltpu.roll(v, 64, axis=v.ndim - 1)


def col_of(shape):
    return lax.broadcasted_iota(jnp.int32, shape, 0) % 16


def from_left(v):
    return jnp.where(col_of(v.shape) == 0, 0.0, pltpu.roll(v, 1, axis=0))


def from_right(v):
    return jnp.where(col_of(v.shape) == 15, 0.0, pltpu.roll(v, v.shape[0] - 1, axis=0))


def split_halves(m):
    low = low_lanes((8, 128))
    zero = jnp.zeros((8, 128), F32)
    halves = ([], [])
    for a in range(3):
        blocks = ([], [])
        for k in range(5):
            t = 9 * a + 2 * k
            even = m[:, t * 128 : (t + 1) * 128]
            odd = m[:, (t + 1) * 128 : (t + 2) * 128] if k < 4 else zero
            blocks[0].append(jnp.where(low, even, swap_lanes(odd)))
            blocks[1].append(jnp.where(low, swap_lanes(even), odd))
        for c in range(2):
            halves[c].append(jnp.concatenate(blocks[c], axis=1))
    return halves


def slot_of(blocks, s):
    return swap_lanes(blocks[s // 2]) if s % 2 else blocks[s // 2]


def outputs_of(z):
    u = []
    for b in range(3):
        z0, z1, z2 = (slot_of(z, 3 * b + e) for e in range(3))
        u.append((from_left(z0) + z1 + z2, z0 + z1 + from_right(z2)))
    out = ([], [])
    for j in range(2):
        common = u[0][j][0:80] + u[2][j][16:96]
        out[0].append(common + u[1][j][16:96])
        out[1].append(common + u[1][j][0:80])
    return out


def folded(g):
    slots = []
    for b in range(3):
        v = []
        for j in range(2):
            g0, g1 = g[0][j], g[1][j]
            v.append((g1[16:80] + g0[16:80], g0[0:64] + g1[16:80], g1[0:64] + g0[0:64])[b])
        slots += [v[1] + from_right(v[0]), v[0] + v[1], from_left(v[1]) + v[0]]
    low = low_lanes((64, 128))
    blocks = []
    for k in range(5):
        odd = swap_lanes(slots[2 * k + 1]) if k < 4 else jnp.zeros((64, 128), F32)
        blocks.append(jnp.where(low, slots[2 * k], odd))
    return blocks


def adam(g, master, first, second, ema):
    new_first = beta_first * first + (1.0 - beta_first) * g
    new_second = beta_second * second + (1.0 - beta_second) * g * g
    new_master = master - learn_rate * new_first / (jnp.sqrt(new_second) + adam_eps)
    new_ema = ema_decay * ema + (1.0 - ema_decay) * new_master
    return new_master, new_first, new_second, new_ema


def remote(src, dst, send_sem, recv_sem, device):
    return pltpu.make_async_remote_copy(
        src_ref=src,
        dst_ref=dst,
        send_sem=send_sem,
        recv_sem=recv_sem,
        device_id=device,
        device_id_type=MESH,
    )


def kernel(
    latent,
    target,
    master,
    first_hbm,
    second_hbm,
    ema_hbm,
    out_master,
    out_first,
    out_second,
    out_ema,
    out_latent,
    out_loss,
    pair_out,
    pair_in,
    weights,
    xe,
    xc,
    te,
    tf,
    tp,
    zs,
    hs,
    dw,
    far_b,
    near_b,
    far_a,
    near_a,
    total,
    zsend_buf,
    zrecv_buf,
    gsend_buf,
    grecv_buf,
    lat_own,
    lat_out,
    lat_in,
    first,
    second,
    ema,
    pair_sem,
    ag_send,
    ag_recv,
    x_send,
    x_recv,
    t_send,
    t_recv,
    rs_send,
    rs_recv,
    z_send,
    z_recv,
    g_send,
    g_recv,
    lat_sem,
    load_sem,
):
    z = lax.axis_index("tm")
    h = lax.axis_index("height")
    c = h % 2
    u = h // 2
    other = 1 - c
    sa, sb = 4 - 3 * c, 1 + 3 * c
    pa = jnp.where(c == 0, u // 4, u % 4)
    pb = jnp.where(c == 0, u % 4, u // 4)

    def unit(da, db):
        return ((pa + da + 4) % 4) * sa + ((pb + db + 4) % 4) * sb

    def dev(chip, core, dz=0):
        return ((z + dz + Z) % Z, chip * 2 + core)

    def hop_a(step):
        return dev(unit(step, 0), c)

    def hop_b(step):
        return dev(unit(0, step), c)

    sibling = dev(u, other)
    above, below = (u + 15) % 16, (u + 1) % 16

    barrier = pltpu.get_barrier_semaphore()
    peers = [hop_a(1), hop_a(-1), hop_b(1), hop_b(-1)]
    for dz in (-1, 0, 1):
        for chip in (above, below):
            for core in range(2):
                peers.append(dev(chip, core, dz))
    for peer in peers:
        pl.semaphore_signal(barrier, inc=1, device_id=peer, device_id_type=MESH)

    def greet(i, carry):
        pl.semaphore_signal(
            barrier, inc=1, device_id=dev(u, (c + i % 2) % 2, i // 2), device_id_type=MESH
        )
        return carry

    lax.fori_loop(1, 2 * Z, greet, 0)

    loads = [
        pltpu.make_async_copy(src, dst, load_sem.at[i])
        for i, (src, dst) in enumerate(((first_hbm, first), (second_hbm, second), (ema_hbm, ema)))
    ]
    for load in loads:
        load.start()

    halves = split_halves(master[...] * SCALE)
    for a in range(3):
        pair_out[a] = jnp.where(c == 0, halves[1][a], halves[0][a])

    pl.semaphore_wait(barrier, len(peers) + 2 * Z - 1)

    sent = []

    def send(*args):
        copy = remote(*args)
        copy.start()
        sent.append(copy)

    def arrived(dst, sem):
        remote(dst, dst, ag_send.at[0], sem, sibling).wait_recv()

    send(pair_out, pair_in, pair_sem.at[0], pair_sem.at[1], sibling)

    own_rows = pl.ds(1 + 2 * c, 2)
    edge = pl.ds(c, 1)
    edge_to = jnp.where(c == 0, above, below)
    edge_row = pl.ds(5 - 5 * c, 1)
    n = 0
    for t, dz in ((0, 1), (1, 0), (2, -1)):
        frames = pl.ds(2 * t, 2)
        for flip in range(2):
            if t == 1 and flip == 0:
                continue
            send(
                latent,
                xe.at[frames, own_rows],
                x_send.at[n],
                x_recv.at[2 * t + c],
                dev(u, (c + flip) % 2, dz),
            )
            n += 1
    for t, dz in ((0, 1), (1, 0), (2, -1)):
        frames = pl.ds(2 * t, 2)
        for core in range(2):
            send(
                latent.at[:, edge],
                xe.at[frames, edge_row],
                x_send.at[n],
                x_recv.at[6 + 2 * t + c],
                dev(edge_to, core, dz),
            )
            n += 1

    arrived(pair_in, pair_sem.at[1])
    for a in range(3):
        mine = jnp.where(c == 0, halves[0][a], halves[1][a])
        theirs = pair_in[a]
        rows = jnp.concatenate(
            [jnp.where(c == 0, mine, theirs), jnp.where(c == 0, theirs, mine)], axis=0
        )
        weights[a, u] = rows.astype(BF16)

    def piece(ref, index, part):
        first_col, width = PARTS[part]
        return ref.at[:, index, :, pl.ds(first_col, width)]

    def spread_unit(hop, index, sem):
        for d, step in enumerate((1, -1)):
            place = weights.at[:, index]
            send(place, place, ag_send.at[sem + d], ag_recv.at[sem + d], hop(step))

    def pass_on(hop, index, sem, d):
        place = piece(weights, index, d)
        send(place, place, ag_send.at[sem + 2 + d], ag_recv.at[sem + 2 + d], hop((1, -1)[d]))

    spread_unit(hop_a, unit(0, 0), 0)
    spread_unit(hop_b, unit(0, 0), 4)

    t_rows = pl.ds(1 + 4 * c, 4)
    n = 0
    for t, dz in ((0, 0), (1, -1)):
        frames = pl.ds(2 * t, 2)
        for flip in range(2):
            if t == 0 and flip == 0:
                continue
            send(
                target,
                te.at[frames, t_rows],
                t_send.at[n],
                t_recv.at[2 * t + c],
                dev(u, (c + flip) % 2, dz),
            )
            n += 1
        for core in range(2):
            send(
                target.at[:, pl.ds(3 * c, 1)],
                te.at[frames, pl.ds(9 - 9 * c, 1)],
                t_send.at[n],
                t_recv.at[4 + 2 * t + c],
                dev(edge_to, core, dz),
            )
            n += 1

    for d, da in ((0, -1), (1, 1)):
        arrived(weights.at[:, unit(da, 0)], ag_recv.at[d])
        pass_on(hop_a, unit(da, 0), 0, d)
        spread_unit(hop_b, unit(da, 0), 8 + 4 * d)
    for d, db in ((0, -1), (1, 1)):
        arrived(weights.at[:, unit(0, db)], ag_recv.at[4 + d])
        pass_on(hop_b, unit(0, db), 4, d)
    for d in range(2):
        arrived(piece(weights, unit(2, 0), d), ag_recv.at[2 + d])
    spread_unit(hop_b, unit(2, 0), 16)

    xe[2:4, own_rows] = latent[...]
    te[0:2, t_rows] = target[...]
    for t in range(3):
        for core in range(2):
            rows = pl.ds(1 + 2 * core, 2)
            if t == 1:
                rows = pl.ds(1 + 2 * other, 2)
                if core == 1:
                    continue
                arrived(xe.at[pl.ds(2, 2), rows], x_recv.at[2 + other])
            else:
                arrived(xe.at[pl.ds(2 * t, 2), rows], x_recv.at[2 * t + core])
        for core in range(2):
            arrived(xe.at[pl.ds(2 * t, 2), pl.ds(5 - 5 * core, 1)], x_recv.at[6 + 2 * t + core])

    for i, (da, sem) in enumerate(((-1, 8), (1, 12))):
        for d, db in ((0, -1), (1, 1)):
            arrived(weights.at[:, unit(da, db)], ag_recv.at[sem + d])
            pass_on(hop_b, unit(da, db), sem, d)

    @pl.when(u == 0)
    def _():
        xe[:, 0] = jnp.zeros((6, 16, 256), BF16)

    @pl.when(u == 15)
    def _():
        xe[:, 5] = jnp.zeros((6, 16, 256), BF16)

    @pl.when(z == 0)
    def _():
        xe[0:2] = jnp.zeros((2, 6, 16, 256), BF16)

    for a in range(3):
        xc[:, :, :, a * 256 : (a + 1) * 256] = xe[a : a + 4]

    for t in range(2):
        if t == 0:
            arrived(te.at[pl.ds(0, 2), pl.ds(1 + 4 * other, 4)], t_recv.at[other])
        else:
            for core in range(2):
                arrived(te.at[pl.ds(2, 2), pl.ds(1 + 4 * core, 4)], t_recv.at[2 + core])
        for core in range(2):
            arrived(te.at[pl.ds(2 * t, 2), pl.ds(9 - 9 * core, 1)], t_recv.at[4 + 2 * t + core])

    def sort_target(f, carry):
        tf[...] = te[f].astype(F32).reshape(320, 128)
        for i in range(2):
            for j in range(2):
                for r in range(5):
                    row = 2 * r + 1 - i
                    v = tf[pl.ds(row * 32 + j, 16, stride=2), :]
                    tp[f, i, j, r * 16 : (r + 1) * 16, :] = jnp.where(c == 0, v, swap_lanes(v))
        return carry

    lax.fori_loop(0, 4, sort_target, 0)

    for d, db in ((0, -1), (1, 1)):
        arrived(weights.at[:, unit(2, db)], ag_recv.at[16 + d])
        pass_on(hop_b, unit(2, db), 16, d)
    for da, sem in ((0, 4), (-1, 8), (1, 12), (2, 16)):
        for d in range(2):
            arrived(piece(weights, unit(da, 2), d), ag_recv.at[sem + 2 + d])

    zs[...] = jnp.dot(
        xc[...].reshape(384, 768), weights[...].reshape(768, WIDE), preferred_element_type=F32
    ).reshape(4, 96, WIDE)

    def frame(f, loss):
        out = outputs_of([zs[f, :, k * 128 : (k + 1) * 128] for k in range(5)])
        row = lax.broadcasted_iota(jnp.int32, (80, 128), 0)
        keep = jnp.logical_or(f < 2, z < Z - 1)
        keep0 = jnp.logical_and(keep, jnp.logical_or(row < 64, u < 15))
        keep1 = jnp.logical_and(keep, jnp.logical_or(row >= 16, u > 0))
        own = jnp.where(f < 2, 1.0, 0.0)
        g = ([], [])
        for i in range(2):
            for j in range(2):
                misfit = out[i][j] - tp[f, i, j]
                counted = misfit[16 * i : 16 * i + 64]
                loss = loss + own * jnp.sum(counted * counted, axis=0, keepdims=True)
                rounded = misfit.astype(BF16).astype(F32)
                g[i].append(jnp.where((keep0, keep1)[i], rounded, 0.0))
        for k, block in enumerate(folded(g)):
            hs[f, :, k * 128 : (k + 1) * 128] = block.astype(BF16)
        return loss

    loss = lax.fori_loop(0, 4, frame, jnp.zeros((1, 128), F32))
    loss = jnp.where(low_lanes((1, 128)), 0.0, swap_lanes(loss))

    x_t = xe[2:4, 1:5].reshape(128, 256).astype(F32).T.astype(BF16)
    for a in range(3):
        grads = hs[2 - a : 4 - a].reshape(128, WIDE)
        part = jnp.dot(x_t, grads, preferred_element_type=F32)
        if a == 0:
            dw[0, :, :, 0:512] = part[:, 0:512].astype(BF16).reshape(16, 16, 512)
            dw[0, :, :, 512:WIDE] = (part[:, 512:WIDE] + loss).astype(BF16).reshape(16, 16, 128)
        else:
            dw[a] = part.astype(BF16).reshape(16, 16, WIDE)

    def open_ring(hop, units, far, near, slot, sem):
        far_unit, plus, minus = units
        for d, step in enumerate((1, -1)):
            first_col, width = PARTS[d]
            send(
                piece(dw, far_unit, d),
                far.at[slot, :, :, pl.ds(first_col, width)],
                rs_send.at[sem + d],
                rs_recv.at[sem + d],
                hop(step),
            )
        for d, (step, index) in enumerate(((1, plus), (-1, minus))):
            first_col, width = PARTS[1 - d]
            send(
                piece(dw, index, 1 - d),
                near.at[slot, d, :, :, pl.ds(first_col, width)],
                rs_send.at[sem + 2 + d],
                rs_recv.at[sem + 2 + d],
                hop(step),
            )

    def add_far(hop, units, far, near, slot, sem):
        _, plus, minus = units
        for d, (step, index) in enumerate(((1, plus), (-1, minus))):
            first_col, width = PARTS[d]
            cols = pl.ds(first_col, width)
            arrived(far.at[slot, :, :, cols], rs_recv.at[sem + d])
            dw[:, index, :, cols] = (
                dw[:, index, :, cols].astype(F32) + far[slot, :, :, cols].astype(F32)
            ).astype(BF16)
            send(
                piece(dw, index, d),
                near.at[slot, d, :, :, cols],
                rs_send.at[sem + 4 + d],
                rs_recv.at[sem + 4 + d],
                hop(step),
            )

    def close_ring(index, near, slot, sem):
        for d in range(2):
            for early in range(2):
                first_col, width = PARTS[1 - d if early else d]
                arrived(
                    near.at[slot, d, :, :, pl.ds(first_col, width)],
                    rs_recv.at[sem + (2 if early else 4) + d],
                )
        return (
            dw[:, index].astype(F32) + near[slot, 0].astype(F32) + near[slot, 1].astype(F32)
        )

    order = (2, 1, -1, 0)
    rings = [(unit(k, 2), unit(k, 1), unit(k, -1)) for k in order]
    for i in range(4):
        open_ring(hop_b, rings[i], far_b, near_b, i, 6 * i)

    lat = jnp.zeros((128, 256), F32)
    for a in range(3):
        lat = lat + lax.dot_general(
            hs[2 - a : 4 - a].reshape(128, WIDE),
            weights[a].reshape(256, WIDE),
            (((1,), (1,)), ((), ())),
            preferred_element_type=F32,
        )
    lat = lat.reshape(2, 4, 16, 256)
    lat_out[...] = jnp.where(c == 0, lat[:, 2:4], lat[:, 0:2])
    lat_own[...] = jnp.where(c == 0, lat[:, 0:2], lat[:, 2:4])
    send(lat_out, lat_in, lat_sem.at[0], lat_sem.at[1], sibling)

    for i in range(4):
        add_far(hop_b, rings[i], far_b, near_b, i, 6 * i)
    for i in range(3):
        dw[:, unit(order[i], 0)] = close_ring(unit(order[i], 0), near_b, i, 6 * i).astype(BF16)
    ring_a = (unit(2, 0), unit(1, 0), unit(-1, 0))
    open_ring(hop_a, ring_a, far_a, near_a, 0, 24)
    dw[:, unit(0, 0)] = close_ring(unit(0, 0), near_b, 3, 18).astype(BF16)
    add_far(hop_a, ring_a, far_a, near_a, 0, 24)
    total[...] = close_ring(unit(0, 0), near_a, 0, 24)

    for p in range(15):
        a, k = p // 5, p % 5
        zsend_buf[p] = total[a, :, k * 128 : (k + 1) * 128].astype(BF16)
    zsend_buf[15] = jnp.zeros((16, 128), BF16)

    def z_copy(i):
        to = (z + i) % Z
        return remote(zsend_buf.at[to], zrecv_buf.at[z], z_send.at[i], z_recv.at[z], (to, h))

    def z_start(i, carry):
        z_copy(i).start()
        return carry

    lax.fori_loop(1, Z, z_start, 0)

    def z_add(i, acc):
        source = (z + i) % Z
        arrived(zrecv_buf.at[source], z_recv.at[source])
        return acc + zrecv_buf[source].astype(F32)

    acc = lax.fori_loop(1, Z, z_add, zsend_buf[z].astype(F32))
    for core in range(2):
        gsend_buf[core] = acc[8 * core : 8 * core + 8]
    grecv_buf[c, z] = gsend_buf[c]

    def g_copy(i):
        core = (c + i % 2) % 2
        return remote(
            gsend_buf.at[core],
            grecv_buf.at[c, z],
            g_send.at[i],
            g_recv.at[c * Z + z],
            dev(u, core, i // 2),
        )

    def g_start(i, carry):
        g_copy(i).start()
        return carry

    lax.fori_loop(1, 2 * Z, g_start, 0)

    arrived(lat_in, lat_sem.at[1])
    out_latent[...] = (lat_own[...] + lat_in[...]).astype(BF16)
    for load in loads:
        load.wait()

    def g_wait(i, carry):
        core = (c + i % 2) % 2
        source = (z + i // 2) % Z
        arrived(grecv_buf.at[core, source], g_recv.at[core * Z + source])
        return carry

    lax.fori_loop(1, 2 * Z, g_wait, 0)

    low = low_lanes((8, 128))
    for a in range(3):
        for k in range(5):
            b0, b1 = grecv_buf[0, 5 * a + k], grecv_buf[1, 5 * a + k]
            pair = (jnp.where(low, b0, swap_lanes(b1)), jnp.where(low, swap_lanes(b0), b1))
            for s in range(2):
                if 2 * k + s == 9:
                    if a == 0:
                        whole = jnp.where(low, 0.0, b0 + b1)[0:1]
                        out_loss[0, 0] = jnp.sum(whole) * (1.0 / 16777216)
                    continue
                cols = pl.ds((9 * a + 2 * k + s) * 128, 128)
                values = adam(
                    SCALE * pair[s], master[:, cols], first[:, cols], second[:, cols], ema[:, cols]
                )
                for ref, value in zip((out_master, out_first, out_second, out_ema), values):
                    ref[:, cols] = value

    for copy in sent:
        copy.wait_send()

    def z_done(i, carry):
        z_copy(i).wait_send()
        return carry

    def g_done(i, carry):
        g_copy(i).wait_send()
        return carry

    lax.fori_loop(1, Z, z_done, 0)
    lax.fori_loop(1, 2 * Z, g_done, 0)


def per_device(latent, target_frames, master, first_moment, second_moment, ema_weights):
    vmem = pl.BlockSpec(memory_space=pltpu.VMEM)
    hbm = pl.BlockSpec(memory_space=pl.ANY)
    state = jax.ShapeDtypeStruct(master.shape, F32)
    dma = pltpu.SemaphoreType.DMA
    outs = pl.pallas_call(
        kernel,
        out_shape=(
            state,
            state,
            state,
            state,
            jax.ShapeDtypeStruct(latent.shape, BF16),
            jax.ShapeDtypeStruct((1, 1), F32),
        ),
        in_specs=[vmem, vmem, vmem, hbm, hbm, hbm],
        out_specs=(vmem, vmem, vmem, vmem, vmem, pl.BlockSpec(memory_space=pltpu.SMEM)),
        scratch_shapes=[
            pltpu.VMEM((3, 8, WIDE), F32),
            pltpu.VMEM((3, 8, WIDE), F32),
            pltpu.VMEM((3, 16, 16, WIDE), BF16),
            pltpu.VMEM((6, 6, 16, 256), BF16),
            pltpu.VMEM((4, 6, 16, 768), BF16),
            pltpu.VMEM((4, 10, 32, 128), BF16),
            pltpu.VMEM((320, 128), F32),
            pltpu.VMEM((4, 2, 2, 80, 128), F32),
            pltpu.VMEM((4, 96, WIDE), F32),
            pltpu.VMEM((4, 64, WIDE), BF16),
            pltpu.VMEM((3, 16, 16, WIDE), BF16),
            pltpu.VMEM((4, 3, 16, WIDE), BF16),
            pltpu.VMEM((4, 2, 3, 16, WIDE), BF16),
            pltpu.VMEM((1, 3, 16, WIDE), BF16),
            pltpu.VMEM((1, 2, 3, 16, WIDE), BF16),
            pltpu.VMEM((3, 16, WIDE), F32),
            pltpu.VMEM((16, 16, 128), BF16),
            pltpu.VMEM((16, 16, 128), BF16),
            pltpu.VMEM((2, 8, 128), F32),
            pltpu.VMEM((2, 16, 8, 128), F32),
            pltpu.VMEM((2, 2, 16, 256), F32),
            pltpu.VMEM((2, 2, 16, 256), F32),
            pltpu.VMEM((2, 2, 16, 256), F32),
            pltpu.VMEM((8, 3456), F32),
            pltpu.VMEM((8, 3456), F32),
            pltpu.VMEM((8, 3456), F32),
            dma((2,)),
            dma((20,)),
            dma((20,)),
            dma((11,)),
            dma((12,)),
            dma((7,)),
            dma((8,)),
            dma((30,)),
            dma((30,)),
            dma((16,)),
            dma((16,)),
            dma((32,)),
            dma((32,)),
            dma((2,)),
            dma((3,)),
        ],
        compiler_params=pltpu.CompilerParams(
            collective_id=0, has_side_effects=True, vmem_limit_bytes=40 * 1024 * 1024
        ),
    )(latent, target_frames, master, first_moment, second_moment, ema_weights)
    return (*outs[:5], outs[5].reshape(()))


def solution(mesh):
    placed = (
        P("tm", "height", None, None),
        P("tm", "height", None, None),
        P("height", None),
        P("height", None),
        P("height", None),
        P("height", None),
    )
    return jax.shard_map(
        per_device,
        mesh=mesh,
        in_specs=placed,
        out_specs=(
            P("height", None),
            P("height", None),
            P("height", None),
            P("height", None),
            P("tm", "height", None, None),
            P(),
        ),
        check_vma=False,
    )
```

```python
import math

import jax
import jax.numpy as jnp
from jax import lax
from jax.experimental import pallas as pl
from jax.experimental.pallas import tpu as pltpu
from jax.sharding import PartitionSpec as P

learn_rate = 0.3
beta_first = 0.9
beta_second = 0.99
ema_decay = 0.9
adam_eps = 1e-08

MESH = pl.DeviceIdType.MESH
F32 = jnp.float32
BF16 = jnp.bfloat16
SCALE = 1.0 / math.sqrt(27 * 256)
WIDE = 640
Z = 16


def low_lanes(shape):
    return lax.broadcasted_iota(jnp.int32, shape, len(shape) - 1) < 64


def swap_lanes(v):
    return pltpu.roll(v, 64, axis=v.ndim - 1)


def col_of(shape):
    return lax.broadcasted_iota(jnp.int32, shape, 0) % 16


def from_left(v):
    return jnp.where(col_of(v.shape) == 0, 0.0, pltpu.roll(v, 1, axis=0))


def from_right(v):
    return jnp.where(col_of(v.shape) == 15, 0.0, pltpu.roll(v, v.shape[0] - 1, axis=0))


def split_halves(m):
    low = low_lanes((8, 128))
    zero = jnp.zeros((8, 128), F32)
    halves = ([], [])
    for a in range(3):
        blocks = ([], [])
        for k in range(5):
            t = 9 * a + 2 * k
            even = m[:, t * 128 : (t + 1) * 128]
            odd = m[:, (t + 1) * 128 : (t + 2) * 128] if k < 4 else zero
            blocks[0].append(jnp.where(low, even, swap_lanes(odd)))
            blocks[1].append(jnp.where(low, swap_lanes(even), odd))
        for c in range(2):
            halves[c].append(jnp.concatenate(blocks[c], axis=1))
    return halves


def slot_of(blocks, s):
    return swap_lanes(blocks[s // 2]) if s % 2 else blocks[s // 2]


def outputs_of(z):
    u = []
    for b in range(3):
        z0, z1, z2 = (slot_of(z, 3 * b + e) for e in range(3))
        u.append((from_left(z0) + z1 + z2, z0 + z1 + from_right(z2)))
    out = ([], [])
    for j in range(2):
        common = u[0][j][0:80] + u[2][j][16:96]
        out[0].append(common + u[1][j][16:96])
        out[1].append(common + u[1][j][0:80])
    return out


def folded(g):
    slots = []
    for b in range(3):
        v = []
        for j in range(2):
            g0, g1 = g[0][j], g[1][j]
            v.append((g1[16:80] + g0[16:80], g0[0:64] + g1[16:80], g1[0:64] + g0[0:64])[b])
        slots += [v[1] + from_right(v[0]), v[0] + v[1], from_left(v[1]) + v[0]]
    low = low_lanes((64, 128))
    blocks = []
    for k in range(5):
        odd = swap_lanes(slots[2 * k + 1]) if k < 4 else jnp.zeros((64, 128), F32)
        blocks.append(jnp.where(low, slots[2 * k], odd))
    return blocks


def remote(src, dst, send_sem, recv_sem, device):
    return pltpu.make_async_remote_copy(
        src_ref=src,
        dst_ref=dst,
        send_sem=send_sem,
        recv_sem=recv_sem,
        device_id=device,
        device_id_type=MESH,
    )


def kernel(
    latent,
    target,
    master,
    out_grad,
    out_own,
    out_other,
    out_loss,
    own_kernel,
    pair_out,
    pair_in,
    weights,
    xe,
    xc,
    te,
    tf,
    tp,
    zs,
    hs,
    dw,
    got_b,
    part_b,
    got_a,
    swap_out,
    swap_in,
    zsend_buf,
    zrecv_buf,
    gsend_buf,
    grecv_buf,
    lat_out,
    pair_sem,
    ag_send,
    ag_recv,
    x_send,
    x_recv,
    t_send,
    t_recv,
    rb_send,
    rb_recv,
    ra_send,
    ra_recv,
    swap_sem,
    z_send,
    z_recv,
    g_send,
    g_recv,
    lat_sem,
    load_sem,
):
    z = lax.axis_index("tm")
    h = lax.axis_index("height")
    c = h % 2
    u = h // 2
    other = 1 - c
    sa, sb = 4 - 3 * c, 1 + 3 * c
    pa = jnp.where(c == 0, u // 4, u % 4)
    pb = jnp.where(c == 0, u % 4, u // 4)

    def unit(da, db):
        return ((pa + da) % 4) * sa + ((pb + db) % 4) * sb

    def dev(chip, core, dz=0):
        return ((z + dz + Z) % Z, chip * 2 + core)

    sibling = dev(u, other)
    above, below = (u + 15) % 16, (u + 1) % 16
    own_rows = pl.ds(1 + 2 * c, 2)
    t_rows = pl.ds(1 + 4 * c, 4)

    loads = [
        pltpu.make_async_copy(src, dst, load_sem.at[i])
        for i, (src, dst) in enumerate(
            ((master, own_kernel), (latent, xe.at[2:4, own_rows]), (target, te.at[0:2, t_rows]))
        )
    ]
    for load in loads:
        load.start()

    barrier = pltpu.get_barrier_semaphore()
    peers = [sibling]
    for j in range(1, 4):
        peers += [dev(unit(j, 0), c), dev(unit(0, j), c)]
    for dz in (-1, 0, 1):
        for chip in (above, below):
            for core in range(2):
                peers.append(dev(chip, core, dz))
        if dz:
            peers.append(dev(u, other, dz))
    for peer in peers:
        pl.semaphore_signal(barrier, inc=1, device_id=peer, device_id_type=MESH)

    def greet(i, carry):
        pl.semaphore_signal(barrier, inc=1, device_id=((z + i) % Z, h), device_id_type=MESH)
        return carry

    lax.fori_loop(1, Z, greet, 0)

    loads[0].wait()
    halves = split_halves(own_kernel[...] * SCALE)
    for a in range(3):
        pair_out[a] = jnp.where(c == 0, halves[1][a], halves[0][a])

    pl.semaphore_wait(barrier, len(peers) + Z - 1)

    sent = []

    def send(*args):
        copy = remote(*args)
        copy.start()
        sent.append(copy)

    def arrived(dst, sem):
        remote(dst, dst, ag_send.at[0], sem, sibling).wait_recv()

    send(pair_out, pair_in, pair_sem.at[0], pair_sem.at[1], sibling)

    edge = pl.ds(c, 1)
    edge_to = jnp.where(c == 0, above, below)
    edge_row = pl.ds(5 - 5 * c, 1)

    def send_latent():
        n = 0
        for t, dz in ((0, 1), (1, 0), (2, -1)):
            frames = pl.ds(2 * t, 2)
            for flip in range(2):
                if t == 1 and flip == 0:
                    continue
                send(
                    latent,
                    xe.at[frames, own_rows],
                    x_send.at[n],
                    x_recv.at[2 * t + c],
                    dev(u, (c + flip) % 2, dz),
                )
                n += 1
        for t, dz in ((0, 1), (1, 0), (2, -1)):
            frames = pl.ds(2 * t, 2)
            for core in range(2):
                send(
                    latent.at[:, edge],
                    xe.at[frames, edge_row],
                    x_send.at[n],
                    x_recv.at[6 + 2 * t + c],
                    dev(edge_to, core, dz),
                )
                n += 1

    def send_target():
        n = 0
        for t, dz in ((0, 0), (1, -1)):
            frames = pl.ds(2 * t, 2)
            for flip in range(2):
                if t == 0 and flip == 0:
                    continue
                send(
                    target,
                    te.at[frames, t_rows],
                    t_send.at[n],
                    t_recv.at[2 * t + c],
                    dev(u, (c + flip) % 2, dz),
                )
                n += 1
            for core in range(2):
                send(
                    target.at[:, pl.ds(3 * c, 1)],
                    te.at[frames, pl.ds(9 - 9 * c, 1)],
                    t_send.at[n],
                    t_recv.at[4 + 2 * t + c],
                    dev(edge_to, core, dz),
                )
                n += 1

    arrived(pair_in, pair_sem.at[1])
    for a in range(3):
        mine = jnp.where(c == 0, halves[0][a], halves[1][a])
        theirs = pair_in[a]
        rows = jnp.concatenate(
            [jnp.where(c == 0, mine, theirs), jnp.where(c == 0, theirs, mine)], axis=0
        )
        weights[a, u] = rows.astype(BF16)

    def send_unit(index, sem, to):
        place = weights.at[:, index]
        send(place, place, ag_send.at[sem], ag_recv.at[sem], dev(to, c))

    far_first = (2, 1, 3)
    for j in far_first:
        send_unit(u, j - 1, unit(j, 0))
    for j in far_first:
        send_unit(u, 2 + j, unit(0, j))
    send_latent()
    for k in (1, 3, 2):
        index = unit(4 - k, 0)
        arrived(weights.at[:, index], ag_recv.at[k - 1])
        for j in far_first:
            send_unit(index, 2 + 3 * k + j, unit(0, j))
    send_target()

    for load in loads[1:]:
        load.wait()
    for t in range(3):
        for core in range(2):
            rows = pl.ds(1 + 2 * core, 2)
            if t == 1:
                rows = pl.ds(1 + 2 * other, 2)
                if core == 1:
                    continue
                arrived(xe.at[pl.ds(2, 2), rows], x_recv.at[2 + other])
            else:
                arrived(xe.at[pl.ds(2 * t, 2), rows], x_recv.at[2 * t + core])
        for core in range(2):
            arrived(xe.at[pl.ds(2 * t, 2), pl.ds(5 - 5 * core, 1)], x_recv.at[6 + 2 * t + core])

    @pl.when(u == 0)
    def _():
        xe[:, 0] = jnp.zeros((6, 16, 256), BF16)

    @pl.when(u == 15)
    def _():
        xe[:, 5] = jnp.zeros((6, 16, 256), BF16)

    @pl.when(z == 0)
    def _():
        xe[0:2] = jnp.zeros((2, 6, 16, 256), BF16)

    for a in range(3):
        xc[:, :, :, a * 256 : (a + 1) * 256] = xe[a : a + 4]
    x_t = xe[2:4, 1:5].reshape(128, 256).astype(F32).T.astype(BF16)

    for t in range(2):
        if t == 0:
            arrived(te.at[pl.ds(0, 2), pl.ds(1 + 4 * other, 4)], t_recv.at[other])
        else:
            for core in range(2):
                arrived(te.at[pl.ds(2, 2), pl.ds(1 + 4 * core, 4)], t_recv.at[2 + core])
        for core in range(2):
            arrived(te.at[pl.ds(2 * t, 2), pl.ds(9 - 9 * core, 1)], t_recv.at[4 + 2 * t + core])

    def sort_target(f, carry):
        tf[...] = te[f].astype(F32).reshape(320, 128)
        for i in range(2):
            for j in range(2):
                for r in range(5):
                    row = 2 * r + 1 - i
                    v = tf[pl.ds(row * 32 + j, 16, stride=2), :]
                    tp[f, i, j, r * 16 : (r + 1) * 16, :] = jnp.where(c == 0, v, swap_lanes(v))
        return carry

    lax.fori_loop(0, 4, sort_target, 0)

    for k in (0, 3, 1, 2):
        for j in far_first:
            arrived(weights.at[:, unit(4 - k, 4 - j)], ag_recv.at[2 + 3 * k + j])

    zs[...] = jnp.dot(
        xc[...].reshape(384, 768), weights[...].reshape(768, WIDE), preferred_element_type=F32
    ).reshape(4, 96, WIDE)

    def frame(f, loss):
        out = outputs_of([zs[f, :, k * 128 : (k + 1) * 128] for k in range(5)])
        row = lax.broadcasted_iota(jnp.int32, (80, 128), 0)
        keep = jnp.logical_or(f < 2, z < Z - 1)
        keep0 = jnp.logical_and(keep, jnp.logical_or(row < 64, u < 15))
        keep1 = jnp.logical_and(keep, jnp.logical_or(row >= 16, u > 0))
        own = jnp.where(f < 2, 1.0, 0.0)
        g = ([], [])
        for i in range(2):
            for j in range(2):
                misfit = out[i][j] - tp[f, i, j]
                counted = misfit[16 * i : 16 * i + 64]
                loss = loss + own * jnp.sum(counted * counted, axis=0, keepdims=True)
                rounded = misfit.astype(BF16).astype(F32)
                g[i].append(jnp.where((keep0, keep1)[i], rounded, 0.0))
        for k, block in enumerate(folded(g)):
            hs[f, :, k * 128 : (k + 1) * 128] = block.astype(BF16)
        return loss

    loss = lax.fori_loop(0, 4, frame, jnp.zeros((1, 128), F32))
    loss = jnp.where(low_lanes((1, 128)), 0.0, swap_lanes(loss))

    for a in range(3):
        grads = hs[2 - a : 4 - a].reshape(128, WIDE)
        part = jnp.dot(x_t, grads, preferred_element_type=F32)
        for v in range(16):
            rows = part[16 * v : 16 * v + 16]
            in_b = jnp.where(c == 0, v % 4, v // 4)
            in_a = jnp.where(c == 0, v // 4, v % 4)
            if a == 0:
                dw[a, in_b, in_a, :, 0:512] = rows[:, 0:512].astype(BF16)
                dw[a, in_b, in_a, :, 512:WIDE] = (rows[:, 512:WIDE] + loss).astype(BF16)
            else:
                dw[a, in_b, in_a] = rows.astype(BF16)
        for j in far_first:
            sem = 3 * a + j - 1
            send(
                dw.at[a, (pb + j) % 4],
                got_b.at[a, j - 1],
                rb_send.at[sem],
                rb_recv.at[sem],
                dev(unit(0, j), c),
            )

    lat = jnp.zeros((128, 256), F32)
    for a in range(3):
        lat = lat + lax.dot_general(
            hs[2 - a : 4 - a].reshape(128, WIDE),
            weights[a].reshape(256, WIDE),
            (((1,), (1,)), ((), ())),
            preferred_element_type=F32,
        )
    lat = lat.reshape(2, 4, 16, 256)
    lat_out[...] = jnp.where(c == 0, lat[:, 2:4], lat[:, 0:2])
    out_own[...] = jnp.where(c == 0, lat[:, 0:2], lat[:, 2:4])
    send(lat_out, out_other, lat_sem.at[0], lat_sem.at[1], sibling)

    for a in range(3):
        for j in range(1, 4):
            arrived(got_b.at[a, j - 1], rb_recv.at[3 * a + j - 1])
        for k in far_first + (0,):
            at = (pa + k) % 4
            rows = dw[a, pb, at].astype(F32)
            for j in range(3):
                rows = rows + got_b[a, j, at].astype(F32)
            part_b[a, k] = rows.astype(BF16)
            if k:
                sem = 3 * a + k - 1
                send(
                    part_b.at[a, k],
                    got_a.at[a, k - 1],
                    ra_send.at[sem],
                    ra_recv.at[sem],
                    dev(unit(k, 0), c),
                )

    totals = []
    for a in range(3):
        rows = part_b[a, 0].astype(F32)
        for j in range(1, 4):
            arrived(got_a.at[a, j - 1], ra_recv.at[3 * a + j - 1])
            rows = rows + got_a[a, j - 1].astype(F32)
        swap_out[a] = jnp.where(c == 0, rows[8:16], rows[0:8])
        totals.append(jnp.where(c == 0, rows[0:8], rows[8:16]))
    send(swap_out, swap_in, swap_sem.at[0], swap_sem.at[1], sibling)
    arrived(swap_in, swap_sem.at[1])

    for a in range(3):
        theirs = swap_in[a]
        rows = jnp.concatenate(
            [jnp.where(c == 0, totals[a], theirs), jnp.where(c == 0, theirs, totals[a])], axis=0
        ).astype(BF16)
        for k in range(5):
            zsend_buf[5 * a + k] = rows[:, k * 128 : (k + 1) * 128]
    zsend_buf[15] = jnp.zeros((16, 128), BF16)

    def z_copy(i):
        to = (z + i) % Z
        return remote(zsend_buf.at[to], zrecv_buf.at[z], z_send.at[i], z_recv.at[z], (to, h))

    def g_copy(i):
        to = (z + i) % Z
        return remote(gsend_buf, grecv_buf.at[z], g_send.at[i], g_recv.at[z], (to, h))

    order = [8] + [v for d in range(7, 0, -1) for v in (d, 16 - d)]
    for i in order:
        z_copy(i).start()

    acc = zsend_buf[z].astype(F32)
    for i in reversed(order):
        source = (z + i) % Z
        arrived(zrecv_buf.at[source], z_recv.at[source])
        acc = acc + zrecv_buf[source].astype(F32)
    gsend_buf[...] = acc.astype(BF16)
    for i in order:
        g_copy(i).start()
    grecv_buf[z] = gsend_buf[...]
    arrived(out_other, lat_sem.at[1])
    for copy in sent:
        copy.wait_send()
    for i in order:
        z_copy(i).wait_send()
    for i in reversed(order):
        source = (z + i) % Z
        arrived(grecv_buf.at[source], g_recv.at[source])

    low = low_lanes((8, 128))
    for a in range(3):
        for k in range(5):
            both = grecv_buf[5 * a + k].astype(F32)
            b0, b1 = both[0:8], both[8:16]
            pair = (jnp.where(low, b0, swap_lanes(b1)), jnp.where(low, swap_lanes(b0), b1))
            for s in range(2):
                if 2 * k + s < 9:
                    t = 9 * a + 2 * k + s
                    out_grad[:, t * 128 : (t + 1) * 128] = SCALE * pair[s]
                elif a == 0:
                    whole = jnp.where(low, 0.0, b0 + b1)[0:1]
                    out_loss[0, 0] = jnp.sum(whole) * (1.0 / 16777216)

    for i in order:
        g_copy(i).wait_send()


def per_device(latent, target_frames, master, first_moment, second_moment, ema_weights):
    vmem = pl.BlockSpec(memory_space=pltpu.VMEM)
    hbm = pl.BlockSpec(memory_space=pltpu.HBM)
    dma = pltpu.SemaphoreType.DMA
    half_grad = jax.ShapeDtypeStruct(latent.shape, F32)
    grad, own, other, loss = pl.pallas_call(
        kernel,
        out_shape=(
            jax.ShapeDtypeStruct(master.shape, F32),
            half_grad,
            half_grad,
            jax.ShapeDtypeStruct((1, 1), F32),
        ),
        in_specs=[hbm, hbm, hbm],
        out_specs=(vmem, vmem, vmem, pl.BlockSpec(memory_space=pltpu.SMEM)),
        scratch_shapes=[
            pltpu.VMEM((8, 3456), F32),
            pltpu.VMEM((3, 8, WIDE), F32),
            pltpu.VMEM((3, 8, WIDE), F32),
            pltpu.VMEM((3, 16, 16, WIDE), BF16),
            pltpu.VMEM((6, 6, 16, 256), BF16),
            pltpu.VMEM((4, 6, 16, 768), BF16),
            pltpu.VMEM((4, 10, 32, 128), BF16),
            pltpu.VMEM((320, 128), F32),
            pltpu.VMEM((4, 2, 2, 80, 128), F32),
            pltpu.VMEM((4, 96, WIDE), F32),
            pltpu.VMEM((4, 64, WIDE), BF16),
            pltpu.VMEM((3, 4, 4, 16, WIDE), BF16),
            pltpu.VMEM((3, 3, 4, 16, WIDE), BF16),
            pltpu.VMEM((3, 4, 16, WIDE), BF16),
            pltpu.VMEM((3, 3, 16, WIDE), BF16),
            pltpu.VMEM((3, 8, WIDE), F32),
            pltpu.VMEM((3, 8, WIDE), F32),
            pltpu.VMEM((16, 16, 128), BF16),
            pltpu.VMEM((16, 16, 128), BF16),
            pltpu.VMEM((16, 128), BF16),
            pltpu.VMEM((16, 16, 128), BF16),
            pltpu.VMEM((2, 2, 16, 256), F32),
            dma((2,)),
            dma((15,)),
            dma((15,)),
            dma((11,)),
            dma((12,)),
            dma((7,)),
            dma((8,)),
            dma((9,)),
            dma((9,)),
            dma((9,)),
            dma((9,)),
            dma((2,)),
            dma((16,)),
            dma((16,)),
            dma((16,)),
            dma((16,)),
            dma((2,)),
            dma((3,)),
        ],
        compiler_params=pltpu.CompilerParams(
            collective_id=0, has_side_effects=True, vmem_limit_bytes=40 * 1024 * 1024
        ),
    )(latent, target_frames, master)
    new_first = beta_first * first_moment + (1.0 - beta_first) * grad
    new_second = beta_second * second_moment + (1.0 - beta_second) * grad * grad
    new_master = master - learn_rate * new_first / (jnp.sqrt(new_second) + adam_eps)
    new_ema = ema_decay * ema_weights + (1.0 - ema_decay) * new_master
    latent_grad = (own + other).astype(BF16)
    return (new_master, new_first, new_second, new_ema, latent_grad, loss.reshape(()))


def solution(mesh):
    placed = (
        P("tm", "height", None, None),
        P("tm", "height", None, None),
        P("height", None),
        P("height", None),
        P("height", None),
        P("height", None),
    )
    return jax.shard_map(
        per_device,
        mesh=mesh,
        in_specs=placed,
        out_specs=(
            P("height", None),
            P("height", None),
            P("height", None),
            P("height", None),
            P("tm", "height", None, None),
            P(),
        ),
        check_vma=False,
    )
```

```python
import math

import jax
import jax.numpy as jnp
from jax import lax
from jax.experimental import pallas as pl
from jax.experimental.pallas import tpu as pltpu
from jax.sharding import PartitionSpec as P

learn_rate = 0.3
beta_first = 0.9
beta_second = 0.99
ema_decay = 0.9
adam_eps = 1e-08

MESH = pl.DeviceIdType.MESH
F32 = jnp.float32
BF16 = jnp.bfloat16
SCALE = 1.0 / math.sqrt(27 * 256)
WIDE = 640
Z = 16


def low_lanes(shape):
    return lax.broadcasted_iota(jnp.int32, shape, len(shape) - 1) < 64


def swap_lanes(v):
    return pltpu.roll(v, 64, axis=v.ndim - 1)


def col_of(shape):
    return lax.broadcasted_iota(jnp.int32, shape, 0) % 16


def from_left(v):
    return jnp.where(col_of(v.shape) == 0, 0.0, pltpu.roll(v, 1, axis=0))


def from_right(v):
    return jnp.where(col_of(v.shape) == 15, 0.0, pltpu.roll(v, v.shape[0] - 1, axis=0))


def split_halves(m):
    low = low_lanes((8, 128))
    zero = jnp.zeros((8, 128), F32)
    halves = ([], [])
    for a in range(3):
        blocks = ([], [])
        for k in range(5):
            t = 9 * a + 2 * k
            even = m[:, t * 128 : (t + 1) * 128]
            odd = m[:, (t + 1) * 128 : (t + 2) * 128] if k < 4 else zero
            blocks[0].append(jnp.where(low, even, swap_lanes(odd)))
            blocks[1].append(jnp.where(low, swap_lanes(even), odd))
        for c in range(2):
            halves[c].append(jnp.concatenate(blocks[c], axis=1))
    return halves


def slot_of(blocks, s):
    return swap_lanes(blocks[s // 2]) if s % 2 else blocks[s // 2]


def outputs_of(z):
    u = []
    for b in range(3):
        z0, z1, z2 = (slot_of(z, 3 * b + e) for e in range(3))
        u.append((from_left(z0) + z1 + z2, z0 + z1 + from_right(z2)))
    out = ([], [])
    for j in range(2):
        common = u[0][j][0:80] + u[2][j][16:96]
        out[0].append(common + u[1][j][16:96])
        out[1].append(common + u[1][j][0:80])
    return out


def folded(g):
    slots = []
    for b in range(3):
        v = []
        for j in range(2):
            g0, g1 = g[0][j], g[1][j]
            v.append((g1[16:80] + g0[16:80], g0[0:64] + g1[16:80], g1[0:64] + g0[0:64])[b])
        slots += [v[1] + from_right(v[0]), v[0] + v[1], from_left(v[1]) + v[0]]
    low = low_lanes((64, 128))
    blocks = []
    for k in range(5):
        odd = swap_lanes(slots[2 * k + 1]) if k < 4 else jnp.zeros((64, 128), F32)
        blocks.append(jnp.where(low, slots[2 * k], odd))
    return blocks


def remote(src, dst, send_sem, recv_sem, device):
    return pltpu.make_async_remote_copy(
        src_ref=src,
        dst_ref=dst,
        send_sem=send_sem,
        recv_sem=recv_sem,
        device_id=device,
        device_id_type=MESH,
    )


def kernel(
    latent,
    target,
    master,
    out_grad,
    out_own,
    out_other,
    out_loss,
    own_kernel,
    pair_out,
    pair_in,
    weights,
    xe,
    xc,
    te,
    tf,
    tp,
    zs,
    hs,
    dw,
    got_b,
    part_b,
    got_a,
    swap_out,
    swap_in,
    zsend_buf,
    zrecv_buf,
    gsend_buf,
    grecv_buf,
    lat_out,
    pair_sem,
    ag_send,
    ag_recv,
    x_send,
    x_recv,
    t_send,
    t_recv,
    rb_send,
    rb_recv,
    ra_send,
    ra_recv,
    swap_sem,
    z_send,
    z_recv,
    g_send,
    g_recv,
    lat_sem,
    load_sem,
    token,
):
    z = lax.axis_index("tm")
    h = lax.axis_index("height")
    c = h % 2
    u = h // 2
    other = 1 - c
    sa, sb = 4 - 3 * c, 1 + 3 * c
    pa = jnp.where(c == 0, u // 4, u % 4)
    pb = jnp.where(c == 0, u % 4, u // 4)

    def unit(da, db):
        return ((pa + da) % 4) * sa + ((pb + db) % 4) * sb

    def dev(chip, core, dz=0):
        return ((z + dz + Z) % Z, chip * 2 + core)

    sibling = dev(u, other)
    above, below = (u + 15) % 16, (u + 1) % 16
    own_rows = pl.ds(1 + 2 * c, 2)
    t_rows = pl.ds(1 + 4 * c, 4)

    loads = [
        pltpu.make_async_copy(src, dst, load_sem.at[i])
        for i, (src, dst) in enumerate(
            ((master, own_kernel), (latent, xe.at[2:4, own_rows]), (target, te.at[0:2, t_rows]))
        )
    ]
    for load in loads:
        load.start()

    barrier = pltpu.get_barrier_semaphore()
    peers = [sibling]
    for j in range(1, 4):
        peers += [dev(unit(j, 0), c), dev(unit(0, j), c)]
    for dz in (-1, 0, 1):
        peers += [dev(above, c, dz), dev(below, c, dz)]
        if dz:
            peers += [dev(u, 0, dz), dev(u, 1, dz)]
    for peer in peers:
        pl.semaphore_signal(barrier, inc=1, device_id=peer, device_id_type=MESH)

    loads[0].wait()
    halves = split_halves(own_kernel[...] * SCALE)
    for a in range(3):
        pair_out[a] = jnp.where(c == 0, halves[1][a], halves[0][a])

    pl.semaphore_wait(barrier, len(peers))

    sent = []

    def send(*args):
        copy = remote(*args)
        copy.start()
        sent.append(copy)

    def arrived(dst, sem):
        remote(dst, dst, ag_send.at[0], sem, sibling).wait_recv()

    def token_out(i):
        for step in (1 << i, -(1 << i)):
            pl.semaphore_signal(
                token.at[i], inc=1, device_id=dev(u, c, step), device_id_type=MESH
            )

    def token_in(i):
        pl.semaphore_wait(token.at[i], 2)

    token_out(0)
    send(pair_out, pair_in, pair_sem.at[0], pair_sem.at[1], sibling)

    edge = pl.ds(c, 1)
    edge_to = jnp.where(c == 0, above, below)
    edge_row = pl.ds(5 - 5 * c, 1)

    def send_latent():
        n = 0
        for t, dz in ((0, 1), (1, 0), (2, -1)):
            frames = pl.ds(2 * t, 2)
            for flip in range(2):
                if t == 1 and flip == 0:
                    continue
                send(
                    latent,
                    xe.at[frames, own_rows],
                    x_send.at[n],
                    x_recv.at[2 * t + c],
                    dev(u, (c + flip) % 2, dz),
                )
                n += 1
        for t, dz in ((0, 1), (1, 0), (2, -1)):
            frames = pl.ds(2 * t, 2)
            send(
                latent.at[:, edge],
                xe.at[frames, edge_row],
                x_send.at[n],
                x_recv.at[6 + 2 * t + c],
                dev(edge_to, c, dz),
            )
            n += 1

    def send_target():
        n = 0
        for t, dz in ((0, 0), (1, -1)):
            frames = pl.ds(2 * t, 2)
            for flip in range(2):
                if t == 0 and flip == 0:
                    continue
                send(
                    target,
                    te.at[frames, t_rows],
                    t_send.at[n],
                    t_recv.at[2 * t + c],
                    dev(u, (c + flip) % 2, dz),
                )
                n += 1
            send(
                target.at[:, pl.ds(3 * c, 1)],
                te.at[frames, pl.ds(9 - 9 * c, 1)],
                t_send.at[n],
                t_recv.at[4 + 2 * t + c],
                dev(edge_to, c, dz),
            )
            n += 1

    arrived(pair_in, pair_sem.at[1])
    for a in range(3):
        mine = jnp.where(c == 0, halves[0][a], halves[1][a])
        theirs = pair_in[a]
        rows = jnp.concatenate(
            [jnp.where(c == 0, mine, theirs), jnp.where(c == 0, theirs, mine)], axis=0
        )
        weights[a, u] = rows.astype(BF16)

    def send_unit(index, sem, to):
        place = weights.at[:, index]
        send(place, place, ag_send.at[sem], ag_recv.at[sem], dev(to, c))

    far_first = (2, 1, 3)
    for j in far_first:
        send_unit(u, j - 1, unit(j, 0))
    for j in far_first:
        send_unit(u, 2 + j, unit(0, j))
    send_latent()
    for k in (1, 3, 2):
        index = unit(4 - k, 0)
        arrived(weights.at[:, index], ag_recv.at[k - 1])
        for j in far_first:
            send_unit(index, 2 + 3 * k + j, unit(0, j))
    token_in(0)
    token_out(1)
    send_target()

    for t in range(3):
        place = xe.at[pl.ds(2 * t, 2), edge_row]
        sem = x_recv.at[6 + 2 * t + c]
        arrived(place, sem)
        send(place, place, x_send.at[8 + t], sem, sibling)
    for t in range(2):
        place = te.at[pl.ds(2 * t, 2), pl.ds(9 - 9 * c, 1)]
        sem = t_recv.at[4 + 2 * t + c]
        arrived(place, sem)
        send(place, place, t_send.at[5 + t], sem, sibling)

    for load in loads[1:]:
        load.wait()
    for t in range(3):
        for core in range(2):
            rows = pl.ds(1 + 2 * core, 2)
            if t == 1:
                rows = pl.ds(1 + 2 * other, 2)
                if core == 1:
                    continue
                arrived(xe.at[pl.ds(2, 2), rows], x_recv.at[2 + other])
            else:
                arrived(xe.at[pl.ds(2 * t, 2), rows], x_recv.at[2 * t + core])
        arrived(xe.at[pl.ds(2 * t, 2), pl.ds(5 - 5 * other, 1)], x_recv.at[6 + 2 * t + other])

    for a in range(3):
        xc[:, :, :, a * 256 : (a + 1) * 256] = xe[a : a + 4]

    @pl.when(u == 0)
    def _():
        xc[:, 0] = jnp.zeros((4, 16, 768), BF16)

    @pl.when(u == 15)
    def _():
        xc[:, 5] = jnp.zeros((4, 16, 768), BF16)

    @pl.when(z == 0)
    def _():
        xc[0:2, :, :, 0:256] = jnp.zeros((2, 6, 16, 256), BF16)
        xc[0:1, :, :, 256:512] = jnp.zeros((1, 6, 16, 256), BF16)

    x_t = xe[2:4, 1:5].reshape(128, 256).astype(F32).T.astype(BF16)

    for t in range(2):
        if t == 0:
            arrived(te.at[pl.ds(0, 2), pl.ds(1 + 4 * other, 4)], t_recv.at[other])
        else:
            for core in range(2):
                arrived(te.at[pl.ds(2, 2), pl.ds(1 + 4 * core, 4)], t_recv.at[2 + core])
        arrived(te.at[pl.ds(2 * t, 2), pl.ds(9 - 9 * other, 1)], t_recv.at[4 + 2 * t + other])

    def sort_target(f, carry):
        tf[...] = te[f].astype(F32).reshape(320, 128)
        for i in range(2):
            for j in range(2):
                for r in range(5):
                    row = 2 * r + 1 - i
                    v = tf[pl.ds(row * 32 + j, 16, stride=2), :]
                    tp[f, i, j, r * 16 : (r + 1) * 16, :] = jnp.where(c == 0, v, swap_lanes(v))
        return carry

    lax.fori_loop(0, 4, sort_target, 0)
    token_in(1)
    token_out(2)

    for k in (0, 3, 1, 2):
        for j in far_first:
            arrived(weights.at[:, unit(4 - k, 4 - j)], ag_recv.at[2 + 3 * k + j])

    zs[...] = jnp.dot(
        xc[...].reshape(384, 768), weights[...].reshape(768, WIDE), preferred_element_type=F32
    ).reshape(4, 96, WIDE)

    def frame(f, loss):
        out = outputs_of([zs[f, :, k * 128 : (k + 1) * 128] for k in range(5)])
        row = lax.broadcasted_iota(jnp.int32, (80, 128), 0)
        keep = jnp.logical_or(f < 2, z < Z - 1)
        keep0 = jnp.logical_and(keep, jnp.logical_or(row < 64, u < 15))
        keep1 = jnp.logical_and(keep, jnp.logical_or(row >= 16, u > 0))
        own = jnp.where(f < 2, 1.0, 0.0)
        g = ([], [])
        for i in range(2):
            for j in range(2):
                misfit = out[i][j] - tp[f, i, j]
                counted = misfit[16 * i : 16 * i + 64]
                loss = loss + own * jnp.sum(counted * counted, axis=0, keepdims=True)
                rounded = misfit.astype(BF16).astype(F32)
                g[i].append(jnp.where((keep0, keep1)[i], rounded, 0.0))
        for k, block in enumerate(folded(g)):
            hs[f, :, k * 128 : (k + 1) * 128] = block.astype(BF16)
        return loss

    loss = lax.fori_loop(0, 4, frame, jnp.zeros((1, 128), F32))
    loss = jnp.where(low_lanes((1, 128)), 0.0, swap_lanes(loss))

    for a in range(3):
        grads = hs[2 - a : 4 - a].reshape(128, WIDE)
        part = jnp.dot(x_t, grads, preferred_element_type=F32)
        for v in range(16):
            rows = part[16 * v : 16 * v + 16]
            in_b = jnp.where(c == 0, v % 4, v // 4)
            in_a = jnp.where(c == 0, v // 4, v % 4)
            if a == 0:
                dw[a, in_b, in_a, :, 0:512] = rows[:, 0:512].astype(BF16)
                dw[a, in_b, in_a, :, 512:WIDE] = (rows[:, 512:WIDE] + loss).astype(BF16)
            else:
                dw[a, in_b, in_a] = rows.astype(BF16)
        for j in far_first:
            sem = 3 * a + j - 1
            send(
                dw.at[a, (pb + j) % 4],
                got_b.at[a, j - 1],
                rb_send.at[sem],
                rb_recv.at[sem],
                dev(unit(0, j), c),
            )

    lat = jnp.zeros((128, 256), F32)
    for a in range(3):
        lat = lat + lax.dot_general(
            hs[2 - a : 4 - a].reshape(128, WIDE),
            weights[a].reshape(256, WIDE),
            (((1,), (1,)), ((), ())),
            preferred_element_type=F32,
        )
    lat = lat.reshape(2, 4, 16, 256)
    lat_out[...] = jnp.where(c == 0, lat[:, 2:4], lat[:, 0:2])
    out_own[...] = jnp.where(c == 0, lat[:, 0:2], lat[:, 2:4])
    send(lat_out, out_other, lat_sem.at[0], lat_sem.at[1], sibling)

    for a in range(3):
        for j in range(1, 4):
            arrived(got_b.at[a, j - 1], rb_recv.at[3 * a + j - 1])
        for k in far_first + (0,):
            at = (pa + k) % 4
            rows = dw[a, pb, at].astype(F32)
            for j in range(3):
                rows = rows + got_b[a, j, at].astype(F32)
            part_b[a, k] = rows.astype(BF16)
            if k:
                sem = 3 * a + k - 1
                send(
                    part_b.at[a, k],
                    got_a.at[a, k - 1],
                    ra_send.at[sem],
                    ra_recv.at[sem],
                    dev(unit(k, 0), c),
                )

    totals = []
    for a in range(3):
        rows = part_b[a, 0].astype(F32)
        for j in range(1, 4):
            arrived(got_a.at[a, j - 1], ra_recv.at[3 * a + j - 1])
            rows = rows + got_a[a, j - 1].astype(F32)
        swap_out[a] = jnp.where(c == 0, rows[8:16], rows[0:8])
        totals.append(jnp.where(c == 0, rows[0:8], rows[8:16]))
    send(swap_out, swap_in, swap_sem.at[0], swap_sem.at[1], sibling)
    arrived(swap_in, swap_sem.at[1])

    for a in range(3):
        theirs = swap_in[a]
        rows = jnp.concatenate(
            [jnp.where(c == 0, totals[a], theirs), jnp.where(c == 0, theirs, totals[a])], axis=0
        ).astype(BF16)
        for k in range(5):
            zsend_buf[5 * a + k] = rows[:, k * 128 : (k + 1) * 128]
    zsend_buf[15] = jnp.zeros((16, 128), BF16)

    def z_copy(i):
        to = (z + i) % Z
        return remote(zsend_buf.at[to], zrecv_buf.at[z], z_send.at[i], z_recv.at[z], (to, h))

    def g_copy(i):
        to = (z + i) % Z
        return remote(gsend_buf, grecv_buf.at[z], g_send.at[i], g_recv.at[z], (to, h))

    token_in(2)
    order = [8] + [v for d in range(7, 0, -1) for v in (d, 16 - d)]
    for i in order:
        z_copy(i).start()

    acc = zsend_buf[z].astype(F32)
    for i in reversed(order):
        source = (z + i) % Z
        arrived(zrecv_buf.at[source], z_recv.at[source])
        acc = acc + zrecv_buf[source].astype(F32)
    gsend_buf[...] = acc.astype(BF16)
    for i in order:
        g_copy(i).start()
    grecv_buf[z] = gsend_buf[...]
    arrived(out_other, lat_sem.at[1])
    for copy in sent:
        copy.wait_send()
    for i in order:
        z_copy(i).wait_send()
    for i in reversed(order):
        source = (z + i) % Z
        arrived(grecv_buf.at[source], g_recv.at[source])

    low = low_lanes((8, 128))
    for a in range(3):
        for k in range(5):
            both = grecv_buf[5 * a + k].astype(F32)
            b0, b1 = both[0:8], both[8:16]
            pair = (jnp.where(low, b0, swap_lanes(b1)), jnp.where(low, swap_lanes(b0), b1))
            for s in range(2):
                if 2 * k + s < 9:
                    t = 9 * a + 2 * k + s
                    out_grad[:, t * 128 : (t + 1) * 128] = SCALE * pair[s]
                elif a == 0:
                    whole = jnp.where(low, 0.0, b0 + b1)[0:1]
                    out_loss[0, 0] = jnp.sum(whole) * (1.0 / 16777216)

    for i in order:
        g_copy(i).wait_send()


def per_device(latent, target_frames, master, first_moment, second_moment, ema_weights):
    vmem = pl.BlockSpec(memory_space=pltpu.VMEM)
    hbm = pl.BlockSpec(memory_space=pltpu.HBM)
    dma = pltpu.SemaphoreType.DMA
    half_grad = jax.ShapeDtypeStruct(latent.shape, F32)
    grad, own, other, loss = pl.pallas_call(
        kernel,
        out_shape=(
            jax.ShapeDtypeStruct(master.shape, F32),
            half_grad,
            half_grad,
            jax.ShapeDtypeStruct((1, 1), F32),
        ),
        in_specs=[hbm, hbm, hbm],
        out_specs=(vmem, vmem, vmem, pl.BlockSpec(memory_space=pltpu.SMEM)),
        scratch_shapes=[
            pltpu.VMEM((8, 3456), F32),
            pltpu.VMEM((3, 8, WIDE), F32),
            pltpu.VMEM((3, 8, WIDE), F32),
            pltpu.VMEM((3, 16, 16, WIDE), BF16),
            pltpu.VMEM((6, 6, 16, 256), BF16),
            pltpu.VMEM((4, 6, 16, 768), BF16),
            pltpu.VMEM((4, 10, 32, 128), BF16),
            pltpu.VMEM((320, 128), F32),
            pltpu.VMEM((4, 2, 2, 80, 128), F32),
            pltpu.VMEM((4, 96, WIDE), F32),
            pltpu.VMEM((4, 64, WIDE), BF16),
            pltpu.VMEM((3, 4, 4, 16, WIDE), BF16),
            pltpu.VMEM((3, 3, 4, 16, WIDE), BF16),
            pltpu.VMEM((3, 4, 16, WIDE), BF16),
            pltpu.VMEM((3, 3, 16, WIDE), BF16),
            pltpu.VMEM((3, 8, WIDE), F32),
            pltpu.VMEM((3, 8, WIDE), F32),
            pltpu.VMEM((16, 16, 128), BF16),
            pltpu.VMEM((16, 16, 128), BF16),
            pltpu.VMEM((16, 128), BF16),
            pltpu.VMEM((16, 16, 128), BF16),
            pltpu.VMEM((2, 2, 16, 256), F32),
            dma((2,)),
            dma((15,)),
            dma((15,)),
            dma((11,)),
            dma((12,)),
            dma((7,)),
            dma((8,)),
            dma((9,)),
            dma((9,)),
            dma((9,)),
            dma((9,)),
            dma((2,)),
            dma((16,)),
            dma((16,)),
            dma((16,)),
            dma((16,)),
            dma((2,)),
            dma((3,)),
            pltpu.SemaphoreType.REGULAR((3,)),
        ],
        compiler_params=pltpu.CompilerParams(
            collective_id=0, has_side_effects=True, vmem_limit_bytes=40 * 1024 * 1024
        ),
    )(*(pltpu.with_memory_space_constraint(v, pltpu.HBM) for v in (latent, target_frames, master)))
    new_first = beta_first * first_moment + (1.0 - beta_first) * grad
    new_second = beta_second * second_moment + (1.0 - beta_second) * grad * grad
    new_master = master - learn_rate * new_first / (jnp.sqrt(new_second) + adam_eps)
    new_ema = ema_decay * ema_weights + (1.0 - ema_decay) * new_master
    latent_grad = (own + other).astype(BF16)
    return (new_master, new_first, new_second, new_ema, latent_grad, loss.reshape(()))


def solution(mesh):
    placed = (
        P("tm", "height", None, None),
        P("tm", "height", None, None),
        P("height", None),
        P("height", None),
        P("height", None),
        P("height", None),
    )
    return jax.shard_map(
        per_device,
        mesh=mesh,
        in_specs=placed,
        out_specs=(
            P("height", None),
            P("height", None),
            P("height", None),
            P("height", None),
            P("tm", "height", None, None),
            P(),
        ),
        check_vma=False,
    )
```

```python
import math

import jax
import jax.numpy as jnp
from jax import lax
from jax.experimental import pallas as pl
from jax.experimental.pallas import tpu as pltpu
from jax.sharding import PartitionSpec as P

learn_rate = 0.3
beta_first = 0.9
beta_second = 0.99
ema_decay = 0.9
adam_eps = 1e-08

MESH = pl.DeviceIdType.MESH
F32 = jnp.float32
BF16 = jnp.bfloat16
SCALE = 1.0 / math.sqrt(27 * 256)
BLOCKS = 7
Z = 16


def group_of(shape):
    return lax.broadcasted_iota(jnp.int32, shape, len(shape) - 1) // 32


def turn(v, groups):
    if isinstance(groups, int) and groups % 4 == 0:
        return v
    return pltpu.roll(v, (groups + 8) % 4 * 32, axis=v.ndim - 1)


def by_group(parts):
    group = group_of(parts[0].shape)
    v = parts[3]
    for i in (2, 1, 0):
        v = jnp.where(group == i, parts[i], v)
    return v


def col_of(shape):
    return lax.broadcasted_iota(jnp.int32, shape, 0) % 16


def from_left(v):
    return jnp.where(col_of(v.shape) == 0, 0.0, pltpu.roll(v, 1, axis=0))


def from_right(v):
    return jnp.where(col_of(v.shape) == 15, 0.0, pltpu.roll(v, v.shape[0] - 1, axis=0))


def quarter_of(m, quarter):
    def tap(a, n, group):
        t = 9 * a + n
        return turn(m[:, t * 128 : (t + 1) * 128], group - quarter)

    blocks = [by_group([tap(a, 4 * k + g, g) for g in range(4)]) for k in range(2) for a in range(3)]
    return blocks + [by_group([tap(g, 8, g) for g in range(3)] + [jnp.zeros((8, 128), F32)])]


def outputs_of(z):
    u = []
    for b in range(3):
        z0, z1, z2 = (turn(z[(3 * b + e) // 4], -((3 * b + e) % 4)) for e in range(3))
        u.append((from_left(z0) + z1 + z2, z0 + z1 + from_right(z2)))
    out = ([], [])
    for j in range(2):
        common = u[0][j][0:80] + u[2][j][16:96]
        out[0].append(common + u[1][j][16:96])
        out[1].append(common + u[1][j][0:80])
    return out


def folded(g):
    slots = []
    for b in range(3):
        v = []
        for j in range(2):
            g0, g1 = g[0][j], g[1][j]
            v.append((g1[16:80] + g0[16:80], g0[0:64] + g1[16:80], g1[0:64] + g0[0:64])[b])
        slots += [v[1] + from_right(v[0]), v[0] + v[1], from_left(v[1]) + v[0]]
    zero = jnp.zeros((64, 128), F32)
    slots += [zero] * 3
    return [by_group([turn(slots[4 * k + g], g) if 4 * k + g < 9 else zero for g in range(4)]) for k in range(3)]


def remote(src, dst, send_sem, recv_sem, device):
    return pltpu.make_async_remote_copy(
        src_ref=src,
        dst_ref=dst,
        send_sem=send_sem,
        recv_sem=recv_sem,
        device_id=device,
        device_id_type=MESH,
    )


def kernel(
    latent,
    target,
    master,
    out_grad,
    out_own,
    out_other,
    out_loss,
    own_kernel,
    pair_out,
    pair_in,
    weights,
    xe,
    xc,
    te,
    tf,
    tp,
    zs,
    hs,
    h9,
    dw,
    got_b,
    part_b,
    got_a,
    swap_out,
    swap_in,
    zsend_buf,
    zrecv_buf,
    gsend_buf,
    grecv_buf,
    lat_out,
    pair_sem,
    ag_send,
    ag_recv,
    x_send,
    x_recv,
    t_send,
    t_recv,
    rb_send,
    rb_recv,
    ra_send,
    ra_recv,
    swap_sem,
    z_send,
    z_recv,
    g_send,
    g_recv,
    lat_sem,
    load_sem,
    token,
):
    z = lax.axis_index("tm")
    h = lax.axis_index("height")
    c = h % 2
    u = h // 2
    s = z % 2
    partner = 1 - 2 * s
    quarter = 2 * s + c
    other = 1 - c
    sa, sb = 4 - 3 * c, 1 + 3 * c
    pa = jnp.where(c == 0, u // 4, u % 4)
    pb = jnp.where(c == 0, u % 4, u // 4)

    def unit(da, db):
        return ((pa + da) % 4) * sa + ((pb + db) % 4) * sb

    def dev(chip, core, dz=0):
        return ((z + dz + Z) % Z, chip * 2 + core)

    sibling = dev(u, other)
    above, below = (u + 15) % 16, (u + 1) % 16
    own_rows = pl.ds(1 + 2 * c, 2)
    t_rows = pl.ds(1 + 4 * c, 4)
    own_x, own_t = pl.ds(2 + 2 * s, 2), pl.ds(2 * s, 2)

    loads = [
        pltpu.make_async_copy(src, dst, load_sem.at[i])
        for i, (src, dst) in enumerate(
            ((master, own_kernel), (latent, xe.at[own_x, own_rows]), (target, te.at[own_t, t_rows]))
        )
    ]
    for load in loads:
        load.start()

    barrier = pltpu.get_barrier_semaphore()
    peers = [sibling]
    for j in range(1, 4):
        peers += [dev(unit(j, 0), c), dev(unit(0, j), c)]
    for dz in (-2, -1, 0, 1, 2):
        peers += [dev(above, c, dz), dev(below, c, dz)]
        if dz:
            peers += [dev(u, 0, dz), dev(u, 1, dz)]
    for peer in peers:
        pl.semaphore_signal(barrier, inc=1, device_id=peer, device_id_type=MESH)

    loads[0].wait()
    scaled = own_kernel[...] * SCALE
    for i, block in enumerate(quarter_of(scaled, 2 * s + other)):
        pair_out[i] = block
    mine = quarter_of(scaled, quarter)

    pl.semaphore_wait(barrier, len(peers))

    sent = []

    def send(*args):
        copy = remote(*args)
        copy.start()
        sent.append(copy)

    def arrived(dst, sem):
        remote(dst, dst, ag_send.at[0], sem, sibling).wait_recv()

    def token_out(i):
        for step in (1 << i, -(1 << i)):
            pl.semaphore_signal(
                token.at[i], inc=1, device_id=dev(u, c, step), device_id_type=MESH
            )

    def token_in(i):
        pl.semaphore_wait(token.at[i], 2)

    token_out(0)
    send(pair_out, pair_in, pair_sem.at[0], pair_sem.at[1], sibling)

    edge = pl.ds(c, 1)
    edge_to = jnp.where(c == 0, above, below)
    edge_row = pl.ds(5 - 5 * c, 1)
    beside = 2 * s - 1
    routes = ((0, 1 + s), (partner, 1 + s), (beside, 3 - 3 * s), (2 * beside, 3 - 3 * s))

    def send_latent():
        n = 0
        for i, (dz, t) in enumerate(routes):
            frames = pl.ds(2 * t, 2)
            for flip in range(2):
                if i or flip:
                    send(
                        latent,
                        xe.at[frames, own_rows],
                        x_send.at[n],
                        x_recv.at[2 * t + c],
                        dev(u, (c + flip) % 2, dz),
                    )
                    n += 1
        for dz, t in routes:
            send(
                latent.at[:, edge],
                xe.at[pl.ds(2 * t, 2), edge_row],
                x_send.at[n],
                x_recv.at[8 + 2 * t + c],
                dev(edge_to, c, dz),
            )
            n += 1

    def target_copies(first, steps, slot):
        copies = []
        frames = pl.ds(2 * slot, 2)
        for dz in steps:
            for flip in range(2):
                if flip or not isinstance(dz, int) or dz:
                    copies.append(
                        remote(
                            target,
                            te.at[frames, t_rows],
                            t_send.at[first + len(copies)],
                            t_recv.at[2 * slot + c],
                            dev(u, (c + flip) % 2, dz),
                        )
                    )
            copies.append(
                remote(
                    target.at[:, pl.ds(3 * c, 1)],
                    te.at[frames, pl.ds(9 - 9 * c, 1)],
                    t_send.at[first + len(copies)],
                    t_recv.at[6 + 2 * slot + c],
                    dev(edge_to, c, dz),
                )
            )
        return copies

    def send_target():
        for copy in target_copies(0, (0, partner), s):
            copy.start()
            sent.append(copy)

        @pl.when(s == 0)
        def _():
            for copy in target_copies(5, (-1, -2), 2):
                copy.start()

    send_latent()
    send_target()

    arrived(pair_in, pair_sem.at[1])
    for i in range(BLOCKS):
        theirs = pair_in[i]
        rows = jnp.concatenate(
            [jnp.where(c == 0, mine[i], theirs), jnp.where(c == 0, theirs, mine[i])], axis=0
        )
        weights[i, u] = rows.astype(BF16)

    def send_unit(index, sem, to):
        place = weights.at[:, index]
        send(place, place, ag_send.at[sem], ag_recv.at[sem], dev(to, c))

    far_first = (2, 1, 3)
    for j in far_first:
        send_unit(u, j - 1, unit(j, 0))
    for j in far_first:
        send_unit(u, 2 + j, unit(0, j))
    for k in (1, 3, 2):
        index = unit(4 - k, 0)
        arrived(weights.at[:, index], ag_recv.at[k - 1])
        for j in far_first:
            send_unit(index, 2 + 3 * k + j, unit(0, j))
    token_in(0)
    token_out(1)

    for t in range(4):
        place = xe.at[pl.ds(2 * t, 2), edge_row]
        arrived(place, x_recv.at[8 + 2 * t + c])
        send(place, place, x_send.at[11 + t], x_recv.at[8 + 2 * t + c], sibling)
    for t in range(3):
        place = te.at[pl.ds(2 * t, 2), pl.ds(9 - 9 * c, 1)]
        arrived(place, t_recv.at[6 + 2 * t + c])
        send(place, place, t_send.at[11 + t], t_recv.at[6 + 2 * t + c], sibling)

    for load in loads[1:]:
        load.wait()
    for t, core in ((0, 0), (0, 1), (3, 0), (3, 1), (2 - s, 0), (2 - s, 1), (1 + s, other)):
        arrived(xe.at[pl.ds(2 * t, 2), pl.ds(1 + 2 * core, 2)], x_recv.at[2 * t + core])
    for t in range(4):
        arrived(xe.at[pl.ds(2 * t, 2), pl.ds(5 - 5 * other, 1)], x_recv.at[8 + 2 * t + other])

    for a in range(3):
        xc[:, :, :, a * 256 : (a + 1) * 256] = xe[a : a + 6]

    @pl.when(u == 0)
    def _():
        xc[:, 0] = jnp.zeros((6, 16, 768), BF16)

    @pl.when(u == 15)
    def _():
        xc[:, 5] = jnp.zeros((6, 16, 768), BF16)

    @pl.when(z < 2)
    def _():
        xc[0:2, :, :, 0:256] = jnp.zeros((2, 6, 16, 256), BF16)
        xc[0:1, :, :, 256:512] = jnp.zeros((1, 6, 16, 256), BF16)

    x_t = xe[2:6, 1:5].reshape(256, 256).astype(F32).T.astype(BF16)

    for t, core in ((2, 0), (2, 1), (1 - s, 0), (1 - s, 1), (s, other)):
        arrived(te.at[pl.ds(2 * t, 2), pl.ds(1 + 4 * core, 4)], t_recv.at[2 * t + core])
    for t in range(3):
        arrived(te.at[pl.ds(2 * t, 2), pl.ds(9 - 9 * other, 1)], t_recv.at[6 + 2 * t + other])

    def sort_target(f, carry):
        tf[...] = te[f].astype(F32).reshape(320, 128)
        for i in range(2):
            for j in range(2):
                for r in range(5):
                    row = 2 * r + 1 - i
                    v = tf[pl.ds(row * 32 + j, 16, stride=2), :]
                    tp[f, i, j, r * 16 : (r + 1) * 16, :] = turn(v, -quarter)
        return carry

    lax.fori_loop(0, 6, sort_target, 0)
    token_in(1)
    token_out(2)

    for k in (0, 3, 1, 2):
        for j in far_first:
            arrived(weights.at[:, unit(4 - k, 4 - j)], ag_recv.at[2 + 3 * k + j])

    ninth = weights[6].reshape(256, 128).astype(F32)
    by_slot = jnp.concatenate(
        [
            weights[0:3].reshape(768, 128),
            weights[3:6].reshape(768, 128),
            jnp.concatenate([turn(ninth, -a).astype(BF16) for a in range(3)], axis=0),
        ],
        axis=1,
    )
    zs[...] = jnp.dot(
        xc[...].reshape(576, 768), by_slot, preferred_element_type=F32
    ).reshape(6, 96, 384)

    def frame(f, loss):
        out = outputs_of([zs[f, :, k * 128 : (k + 1) * 128] for k in range(3)])
        row = lax.broadcasted_iota(jnp.int32, (80, 128), 0)
        keep = jnp.logical_or(f < 4, z < Z - 2)
        keep0 = jnp.logical_and(keep, jnp.logical_or(row < 64, u < 15))
        keep1 = jnp.logical_and(keep, jnp.logical_or(row >= 16, u > 0))
        own = jnp.where(f < 4, 1.0, 0.0)
        g = ([], [])
        for i in range(2):
            for j in range(2):
                misfit = out[i][j] - tp[f, i, j]
                counted = misfit[16 * i : 16 * i + 64]
                loss = loss + own * jnp.sum(counted * counted, axis=0, keepdims=True)
                rounded = misfit.astype(BF16).astype(F32)
                g[i].append(jnp.where((keep0, keep1)[i], rounded, 0.0))
        blocks = folded(g)
        for k in range(2):
            hs[f, :, k * 128 : (k + 1) * 128] = blocks[k].astype(BF16)
        h9[f] = blocks[2]
        return loss

    chunks = ((0, 2), (2, 2), (4, 3))

    def kernel_gradient(i):
        a = 2 - i
        first, n = chunks[i]
        part = jnp.dot(x_t, hs[2 - a : 6 - a].reshape(256, 256), preferred_element_type=F32)
        parts = [part[:, 0:128], part[:, 128:256]]
        if n == 3:
            parts.append(jnp.dot(x_t, ninths(), preferred_element_type=F32) + loss)
        for v in range(16):
            in_b = jnp.where(c == 0, v % 4, v // 4)
            in_a = jnp.where(c == 0, v // 4, v % 4)
            for k in range(n):
                dw[first + k, in_b, in_a] = parts[k][16 * v : 16 * v + 16].astype(BF16)
        for j in far_first:
            sem = 3 * i + j - 1
            send(
                dw.at[pl.ds(first, n), (pb + j) % 4],
                got_b.at[pl.ds(first, n), j - 1],
                rb_send.at[sem],
                rb_recv.at[sem],
                dev(unit(0, j), c),
            )

    def ninths():
        v = h9[2:6].reshape(256, 128)
        for a in (1, 2):
            v = v + turn(h9[2 - a : 6 - a].reshape(256, 128), a)
        return v.astype(BF16)

    loss = lax.fori_loop(0, 4, frame, jnp.zeros((1, 128), F32))
    loss = jnp.where(group_of((1, 128)) == 3, turn(loss, 3), 0.0)
    kernel_gradient(0)
    for i in (1, 2):
        frame(3 + i, jnp.zeros((1, 128), F32))
        kernel_gradient(i)

    over_last = (((1,), (1,)), ((), ()))
    lat = lax.dot_general(
        ninths(), weights[6].reshape(256, 128), over_last, preferred_element_type=F32
    )
    for a in range(3):
        both = jnp.concatenate(
            [weights[a].reshape(256, 128), weights[3 + a].reshape(256, 128)], axis=1
        )
        lat = lat + lax.dot_general(
            hs[2 - a : 6 - a].reshape(256, 256), both, over_last, preferred_element_type=F32
        )
    lat = lat.reshape(4, 4, 16, 256)
    for i in range(2):
        for core in range(2):
            lat_out[i, core] = lat[2 * i : 2 * i + 2, 2 * core : 2 * core + 2]
    out_own[...] = lat_out[s, c]
    for i, (dz, side, core) in enumerate(((0, s, other), (partner, 1 - s, c), (partner, 1 - s, other))):
        send(
            lat_out.at[side, core],
            out_other.at[i],
            lat_sem.at[i],
            lat_sem.at[3 + i],
            dev(u, core, dz),
        )

    kept = {}

    def axis_a(i):
        first, n = chunks[i]
        part = pl.ds(first, n)
        for j in range(1, 4):
            arrived(got_b.at[part, j - 1], rb_recv.at[3 * i + j - 1])
        for k in far_first + (0,):
            at = (pa + k) % 4
            rows = dw[part, pb, at].astype(F32)
            for j in range(3):
                rows = rows + got_b[part, j, at].astype(F32)
            part_b[part, k] = rows.astype(BF16)
            if k:
                sem = 3 * i + k - 1
                send(
                    part_b.at[part, k],
                    got_a.at[part, k - 1],
                    ra_send.at[sem],
                    ra_recv.at[sem],
                    dev(unit(k, 0), c),
                )

    def swap(i):
        first, n = chunks[i]
        part = pl.ds(first, n)
        rows = part_b[part, 0].astype(F32)
        for j in range(1, 4):
            arrived(got_a.at[part, j - 1], ra_recv.at[3 * i + j - 1])
            rows = rows + got_a[part, j - 1].astype(F32)
        swap_out[part] = jnp.where(c == 0, rows[:, 8:16], rows[:, 0:8])
        kept[i] = jnp.where(c == 0, rows[:, 0:8], rows[:, 8:16])
        send(swap_out.at[part], swap_in.at[part], swap_sem.at[i], swap_sem.at[3 + i], sibling)

    def z_block(p):
        return remote(
            zsend_buf.at[p], zrecv_buf.at[z // 2], z_send.at[p], z_recv.at[z // 2], (2 * p + s, h)
        )

    def along_z(i):
        first, n = chunks[i]
        part = pl.ds(first, n)
        arrived(swap_in.at[part], swap_sem.at[3 + i])
        theirs = swap_in[part]
        zsend_buf[part] = jnp.concatenate(
            [jnp.where(c == 0, kept[i], theirs), jnp.where(c == 0, theirs, kept[i])], axis=1
        ).astype(BF16)
        for p in range(first, first + n):

            @pl.when(z // 2 != p)
            def _():
                z_block(p).start()

    axis_a(0)
    axis_a(1)
    swap(0)
    axis_a(2)
    token_in(2)
    along_z(0)
    swap(1)
    along_z(1)
    swap(2)
    along_z(2)

    def g_copy(i):
        to = (z + i) % Z
        return remote(gsend_buf, grecv_buf.at[z], g_send.at[i], g_recv.at[z], (to, h))

    order = [8] + [v for d in range(7, 0, -1) for v in (d, 16 - d)]

    @pl.when(z < 14)
    def _():
        acc = zsend_buf[z // 2].astype(F32)
        for i in (1, 7, 2, 6, 3, 5, 4):
            source = (z // 2 + i) % 8
            arrived(zrecv_buf.at[source], z_recv.at[source])
            acc = acc + zrecv_buf[source].astype(F32)
        gsend_buf[...] = acc.astype(BF16)
        for i in order:
            g_copy(i).start()
        grecv_buf[z] = gsend_buf[...]

    for i in range(3):
        arrived(out_other.at[i], lat_sem.at[3 + i])
    for copy in sent:
        copy.wait_send()
    @pl.when(s == 0)
    def _():
        for copy in target_copies(5, (-1, -2), 2):
            copy.wait_send()

    for p in range(BLOCKS):

        @pl.when(z // 2 != p)
        def _():
            z_block(p).wait_send()

    def grad_tap(t, pieces, group):
        out_grad[:, t * 128 : (t + 1) * 128] = SCALE * by_group(
            [turn(pieces[q], q - group) for q in range(4)]
        )

    for p in range(BLOCKS):
        pieces = []
        for i in range(2):
            at = 2 * p + i

            @pl.when(z != at)
            def _():
                arrived(grecv_buf.at[at], g_recv.at[at])

            both = grecv_buf[at].astype(F32)
            pieces += [both[0:8], both[8:16]]
        for g in range(4):
            if p < 6:
                grad_tap(9 * (2 - p // 2) + 4 * (p % 2) + g, pieces, g)
            elif g < 3:
                grad_tap(9 * g + 8, pieces, g)
    whole = (pieces[0] + pieces[1] + pieces[2] + pieces[3])[0:1]
    whole = jnp.where(group_of((1, 128)) == 3, whole, 0.0)
    out_loss[0, 0] = jnp.sum(whole) * (1.0 / 16777216)

    @pl.when(z < 14)
    def _():
        for i in order:
            g_copy(i).wait_send()


def per_device(latent, target_frames, master, first_moment, second_moment, ema_weights):
    vmem = pl.BlockSpec(memory_space=pltpu.VMEM)
    hbm = pl.BlockSpec(memory_space=pltpu.HBM)
    dma = pltpu.SemaphoreType.DMA
    quarter_grad = jax.ShapeDtypeStruct(latent.shape, F32)
    grad, own, other, loss = pl.pallas_call(
        kernel,
        out_shape=(
            jax.ShapeDtypeStruct(master.shape, F32),
            quarter_grad,
            jax.ShapeDtypeStruct((3, *latent.shape), F32),
            jax.ShapeDtypeStruct((1, 1), F32),
        ),
        in_specs=[hbm, hbm, hbm],
        out_specs=(vmem, vmem, vmem, pl.BlockSpec(memory_space=pltpu.SMEM)),
        scratch_shapes=[
            pltpu.VMEM((8, 3456), F32),
            pltpu.VMEM((BLOCKS, 8, 128), F32),
            pltpu.VMEM((BLOCKS, 8, 128), F32),
            pltpu.VMEM((BLOCKS, 16, 16, 128), BF16),
            pltpu.VMEM((8, 6, 16, 256), BF16),
            pltpu.VMEM((6, 6, 16, 768), BF16),
            pltpu.VMEM((6, 10, 32, 128), BF16),
            pltpu.VMEM((320, 128), F32),
            pltpu.VMEM((6, 2, 2, 80, 128), F32),
            pltpu.VMEM((6, 96, 384), F32),
            pltpu.VMEM((6, 64, 256), BF16),
            pltpu.VMEM((6, 64, 128), F32),
            pltpu.VMEM((BLOCKS, 4, 4, 16, 128), BF16),
            pltpu.VMEM((BLOCKS, 3, 4, 16, 128), BF16),
            pltpu.VMEM((BLOCKS, 4, 16, 128), BF16),
            pltpu.VMEM((BLOCKS, 3, 16, 128), BF16),
            pltpu.VMEM((BLOCKS, 8, 128), F32),
            pltpu.VMEM((BLOCKS, 8, 128), F32),
            pltpu.VMEM((BLOCKS, 16, 128), BF16),
            pltpu.VMEM((8, 16, 128), BF16),
            pltpu.VMEM((16, 128), BF16),
            pltpu.VMEM((16, 16, 128), BF16),
            pltpu.VMEM((2, 2, 2, 2, 16, 256), F32),
            dma((2,)),
            dma((15,)),
            dma((15,)),
            dma((15,)),
            dma((16,)),
            dma((14,)),
            dma((12,)),
            dma((9,)),
            dma((9,)),
            dma((9,)),
            dma((9,)),
            dma((6,)),
            dma((8,)),
            dma((8,)),
            dma((16,)),
            dma((16,)),
            dma((6,)),
            dma((3,)),
            pltpu.SemaphoreType.REGULAR((3,)),
        ],
        compiler_params=pltpu.CompilerParams(
            collective_id=0, has_side_effects=True, vmem_limit_bytes=40 * 1024 * 1024
        ),
    )(*(pltpu.with_memory_space_constraint(v, pltpu.HBM) for v in (latent, target_frames, master)))
    new_first = beta_first * first_moment + (1.0 - beta_first) * grad
    new_second = beta_second * second_moment + (1.0 - beta_second) * grad * grad
    new_master = master - learn_rate * new_first / (jnp.sqrt(new_second) + adam_eps)
    new_ema = ema_decay * ema_weights + (1.0 - ema_decay) * new_master
    latent_grad = (own + other[0] + other[1] + other[2]).astype(BF16)
    return (new_master, new_first, new_second, new_ema, latent_grad, loss.reshape(()))


def solution(mesh):
    placed = (
        P("tm", "height", None, None),
        P("tm", "height", None, None),
        P("height", None),
        P("height", None),
        P("height", None),
        P("height", None),
    )
    return jax.shard_map(
        per_device,
        mesh=mesh,
        in_specs=placed,
        out_specs=(
            P("height", None),
            P("height", None),
            P("height", None),
            P("height", None),
            P("tm", "height", None, None),
            P(),
        ),
        check_vma=False,
    )
```

```python
import math

import jax
import jax.numpy as jnp
from jax import lax
from jax.experimental import pallas as pl
from jax.experimental.pallas import tpu as pltpu
from jax.sharding import PartitionSpec as P

learn_rate = 0.3
beta_first = 0.9
beta_second = 0.99
ema_decay = 0.9
adam_eps = 1e-08

MESH = pl.DeviceIdType.MESH
F32 = jnp.float32
BF16 = jnp.bfloat16
SCALE = 1.0 / math.sqrt(27 * 256)
BLOCKS = 7
Z = 16


def group_of(shape):
    return lax.broadcasted_iota(jnp.int32, shape, len(shape) - 1) // 32


def turn(v, groups):
    if isinstance(groups, int) and groups % 4 == 0:
        return v
    return pltpu.roll(v, (groups + 8) % 4 * 32, axis=v.ndim - 1)


def by_group(parts):
    group = group_of(parts[0].shape)
    v = parts[3]
    for i in (2, 1, 0):
        v = jnp.where(group == i, parts[i], v)
    return v


def col_of(shape):
    return lax.broadcasted_iota(jnp.int32, shape, 0) % 16


def from_left(v):
    return jnp.where(col_of(v.shape) == 0, 0.0, pltpu.roll(v, 1, axis=0))


def from_right(v):
    return jnp.where(col_of(v.shape) == 15, 0.0, pltpu.roll(v, v.shape[0] - 1, axis=0))


def quarter_of(m, quarter):
    def tap(a, n, group):
        t = 9 * a + n
        return turn(m[:, t * 128 : (t + 1) * 128], group - quarter)

    blocks = [by_group([tap(a, 4 * k + g, g) for g in range(4)]) for k in range(2) for a in range(3)]
    return blocks + [by_group([tap(g, 8, g) for g in range(3)] + [jnp.zeros((8, 128), F32)])]


def outputs_of(z):
    u = []
    for b in range(3):
        z0, z1, z2 = (turn(z[(3 * b + e) // 4], -((3 * b + e) % 4)) for e in range(3))
        u.append((from_left(z0) + z1 + z2, z0 + z1 + from_right(z2)))
    out = ([], [])
    for j in range(2):
        common = u[0][j][0:80] + u[2][j][16:96]
        out[0].append(common + u[1][j][16:96])
        out[1].append(common + u[1][j][0:80])
    return out


def folded(g):
    slots = []
    for b in range(3):
        v = []
        for j in range(2):
            g0, g1 = g[0][j], g[1][j]
            v.append((g1[16:80] + g0[16:80], g0[0:64] + g1[16:80], g1[0:64] + g0[0:64])[b])
        slots += [v[1] + from_right(v[0]), v[0] + v[1], from_left(v[1]) + v[0]]
    zero = jnp.zeros((64, 128), F32)
    slots += [zero] * 3
    return [by_group([turn(slots[4 * k + g], g) if 4 * k + g < 9 else zero for g in range(4)]) for k in range(3)]


def remote(src, dst, send_sem, recv_sem, device):
    return pltpu.make_async_remote_copy(
        src_ref=src,
        dst_ref=dst,
        send_sem=send_sem,
        recv_sem=recv_sem,
        device_id=device,
        device_id_type=MESH,
    )


def kernel(
    latent,
    target,
    master,
    out_grad,
    out_own,
    out_other,
    out_loss,
    own_kernel,
    pair_out,
    pair_in,
    weights,
    xe,
    xc,
    te,
    tf,
    tpack,
    epack,
    tq,
    eq,
    tp,
    zs,
    hs,
    h9,
    dw,
    got_b,
    part_b,
    got_a,
    swap_out,
    swap_in,
    zsend_buf,
    zrecv_buf,
    gsend_buf,
    grecv_buf,
    lat_out,
    pair_sem,
    ag_send,
    ag_recv,
    x_send,
    x_recv,
    t_send,
    t_recv,
    rb_send,
    rb_recv,
    ra_send,
    ra_recv,
    swap_sem,
    z_send,
    z_recv,
    g_send,
    g_recv,
    lat_sem,
    load_sem,
    token,
):
    z = lax.axis_index("tm")
    h = lax.axis_index("height")
    c = h % 2
    u = h // 2
    s = z % 2
    partner = 1 - 2 * s
    quarter = 2 * s + c
    other = 1 - c
    sa, sb = 4 - 3 * c, 1 + 3 * c
    pa = jnp.where(c == 0, u // 4, u % 4)
    pb = jnp.where(c == 0, u % 4, u // 4)

    def unit(da, db):
        return ((pa + da) % 4) * sa + ((pb + db) % 4) * sb

    def dev(chip, core, dz=0):
        return ((z + dz + Z) % Z, chip * 2 + core)

    sibling = dev(u, other)
    above, below = (u + 15) % 16, (u + 1) % 16
    own_rows = pl.ds(1 + 2 * c, 2)
    own_x = pl.ds(2 + 2 * s, 2)

    loads = [
        pltpu.make_async_copy(src, dst, load_sem.at[i])
        for i, (src, dst) in enumerate(
            ((master, own_kernel), (latent, xe.at[own_x, own_rows]), (target, te))
        )
    ]
    for load in loads:
        load.start()

    barrier = pltpu.get_barrier_semaphore()
    peers = [sibling]
    for j in range(1, 4):
        peers += [dev(unit(j, 0), c), dev(unit(0, j), c)]
    for dz in (-2, -1, 0, 1, 2):
        peers += [dev(above, c, dz), dev(below, c, dz)]
        if dz:
            peers += [dev(u, 0, dz), dev(u, 1, dz)]
    for peer in peers:
        pl.semaphore_signal(barrier, inc=1, device_id=peer, device_id_type=MESH)

    loads[0].wait()
    scaled = own_kernel[...] * SCALE
    for i, block in enumerate(quarter_of(scaled, 2 * s + other)):
        pair_out[i] = block
    mine = quarter_of(scaled, quarter)

    pl.semaphore_wait(barrier, len(peers))

    sent = []

    def send(*args):
        copy = remote(*args)
        copy.start()
        sent.append(copy)

    def arrived(dst, sem):
        remote(dst, dst, ag_send.at[0], sem, sibling).wait_recv()

    def token_out(i):
        for step in (1 << i, -(1 << i)):
            pl.semaphore_signal(
                token.at[i], inc=1, device_id=dev(u, c, step), device_id_type=MESH
            )

    def token_in(i):
        pl.semaphore_wait(token.at[i], 2)

    token_out(0)
    send(pair_out, pair_in, pair_sem.at[0], pair_sem.at[1], sibling)

    edge = pl.ds(c, 1)
    edge_to = jnp.where(c == 0, above, below)
    edge_row = pl.ds(5 - 5 * c, 1)
    beside = 2 * s - 1
    routes = ((0, 1 + s), (partner, 1 + s), (beside, 3 - 3 * s), (2 * beside, 3 - 3 * s))

    def send_latent():
        n = 0
        for i, (dz, t) in enumerate(routes):
            send(
                latent,
                xe.at[pl.ds(2 * t, 2), own_rows],
                x_send.at[n],
                x_recv.at[2 * t + c],
                dev(u, c if i else other, dz),
            )
            n += 1
        for dz, t in routes:
            send(
                latent.at[:, edge],
                xe.at[pl.ds(2 * t, 2), edge_row],
                x_send.at[n],
                x_recv.at[8 + 2 * t + c],
                dev(edge_to, c, dz),
            )
            n += 1

    def pack_target():
        tf[...] = te[...].astype(F32).reshape(256, 128)
        edges = []
        for f in range(2):
            for j in range(2):
                rows = [tf[pl.ds((4 * f + r) * 32 + j, 16, stride=2), :] for r in range(4)]
                for q in range(4):
                    tpack[q, f, j] = by_group([turn(rows[r], r - q) for r in range(4)]).astype(BF16)
                edges.append(jnp.where(c == 0, rows[0], rows[3]))
        for q in range(4):
            epack[q] = by_group([turn(edges[g], g - q) for g in range(4)]).astype(BF16)
        tq[s, c] = tpack[quarter]

    def target_copies(first, steps, slot):
        copies = []

        def add(src, dst, recv_sem, device):
            copies.append(remote(src, dst, t_send.at[first + len(copies)], recv_sem, device))

        for dz, side in steps:
            near = isinstance(dz, int) and dz == 0
            for core in (other,) if near else (c, other):
                add(tpack.at[2 * side + core], tq.at[slot, c], t_recv.at[2 * slot + c], dev(u, core, dz))
            add(
                epack.at[pl.ds(2 * side, 2)],
                eq.at[slot, c],
                t_recv.at[6 + 2 * slot + c],
                dev(edge_to, c, dz),
            )
        return copies

    def late_copies():
        return target_copies(5, ((-1, 1), (-2, 0)), 2)

    def send_target():
        for copy in target_copies(0, ((0, s), (partner, 1 - s)), s):
            copy.start()
            sent.append(copy)

        @pl.when(s == 0)
        def _():
            for copy in late_copies():
                copy.start()

    loads[2].wait()
    pack_target()

    arrived(pair_in, pair_sem.at[1])
    for i in range(BLOCKS):
        theirs = pair_in[i]
        rows = jnp.concatenate(
            [jnp.where(c == 0, mine[i], theirs), jnp.where(c == 0, theirs, mine[i])], axis=0
        )
        weights[i, u] = rows.astype(BF16)

    def send_unit(index, sem, to):
        place = weights.at[:, index]
        send(place, place, ag_send.at[sem], ag_recv.at[sem], dev(to, c))

    far_first = (2, 1, 3)
    for j in far_first:
        send_unit(u, j - 1, unit(j, 0))
    for j in far_first:
        send_unit(u, 2 + j, unit(0, j))
    send_latent()
    send_target()
    for k in (1, 3, 2):
        index = unit(4 - k, 0)
        arrived(weights.at[:, index], ag_recv.at[k - 1])
        for j in far_first:
            send_unit(index, 2 + 3 * k + j, unit(0, j))
    token_in(0)
    token_out(1)

    def hand_on(place, send_sem, recv_sem):
        arrived(place, recv_sem)
        send(place, place, send_sem, recv_sem, sibling)

    for n, t in enumerate((2 - s, 3, 0)):
        hand_on(xe.at[pl.ds(2 * t, 2), own_rows], x_send.at[12 + n], x_recv.at[2 * t + c])
    for t in range(4):
        hand_on(xe.at[pl.ds(2 * t, 2), edge_row], x_send.at[8 + t], x_recv.at[8 + 2 * t + c])
    for t in range(3):
        recv_sem = t_recv.at[6 + 2 * t + c]
        arrived(eq.at[t, c], recv_sem)
        place = eq.at[t, c, other]
        send(place, place, t_send.at[11 + t], recv_sem, sibling)

    loads[1].wait()
    for t in range(4):
        arrived(xe.at[pl.ds(2 * t, 2), pl.ds(1 + 2 * other, 2)], x_recv.at[2 * t + other])
        arrived(xe.at[pl.ds(2 * t, 2), pl.ds(5 - 5 * other, 1)], x_recv.at[8 + 2 * t + other])

    for a in range(3):
        xc[:, :, :, a * 256 : (a + 1) * 256] = xe[a : a + 6]

    @pl.when(u == 0)
    def _():
        xc[:, 0] = jnp.zeros((6, 16, 768), BF16)

    @pl.when(u == 15)
    def _():
        xc[:, 5] = jnp.zeros((6, 16, 768), BF16)

    @pl.when(z < 2)
    def _():
        xc[0:2, :, :, 0:256] = jnp.zeros((2, 6, 16, 256), BF16)
        xc[0:1, :, :, 256:512] = jnp.zeros((1, 6, 16, 256), BF16)

    x_t = xe[2:6, 1:5].reshape(256, 256).astype(F32).T.astype(BF16)

    for t, core in ((1 - s, c), (2, c), (0, other), (1, other), (2, other)):
        arrived(tq.at[t, core], t_recv.at[2 * t + core])
    for t in range(3):
        arrived(eq.at[t, other, c], t_recv.at[6 + 2 * t + other])

    for t in range(3):
        edges = [eq[t, core, c].astype(F32) for core in range(2)]
        for f in range(2):
            for j in range(2):
                at = 2 * t + f
                tp[at, 0, j, 64:80] = turn(edges[0], -(2 * f + j))
                tp[at, 1, j, 0:16] = turn(edges[1], -(2 * f + j))
                for core in range(2):
                    rows = tq[t, core, f, j].astype(F32)
                    for r in range(2):
                        for i in range(2):
                            k = 16 * (2 * core + r + i)
                            tp[at, i, j, k : k + 16] = turn(rows, -(2 * r + i))
    token_in(1)
    token_out(2)

    for k in (0, 3, 1, 2):
        for j in far_first:
            arrived(weights.at[:, unit(4 - k, 4 - j)], ag_recv.at[2 + 3 * k + j])

    ninth = weights[6].reshape(256, 128).astype(F32)
    by_slot = jnp.concatenate(
        [
            weights[0:3].reshape(768, 128),
            weights[3:6].reshape(768, 128),
            jnp.concatenate([turn(ninth, -a).astype(BF16) for a in range(3)], axis=0),
        ],
        axis=1,
    )
    zs[...] = jnp.dot(
        xc[...].reshape(576, 768), by_slot, preferred_element_type=F32
    ).reshape(6, 96, 384)

    def frame(f, loss):
        out = outputs_of([zs[f, :, k * 128 : (k + 1) * 128] for k in range(3)])
        row = lax.broadcasted_iota(jnp.int32, (80, 128), 0)
        keep = jnp.logical_or(f < 4, z < Z - 2)
        keep0 = jnp.logical_and(keep, jnp.logical_or(row < 64, u < 15))
        keep1 = jnp.logical_and(keep, jnp.logical_or(row >= 16, u > 0))
        own = jnp.where(f < 4, 1.0, 0.0)
        g = ([], [])
        for i in range(2):
            for j in range(2):
                misfit = out[i][j] - tp[f, i, j]
                counted = misfit[16 * i : 16 * i + 64]
                loss = loss + own * jnp.sum(counted * counted, axis=0, keepdims=True)
                rounded = misfit.astype(BF16).astype(F32)
                g[i].append(jnp.where((keep0, keep1)[i], rounded, 0.0))
        blocks = folded(g)
        for k in range(2):
            hs[f, :, k * 128 : (k + 1) * 128] = blocks[k].astype(BF16)
        h9[f] = blocks[2]
        return loss

    chunks = ((0, 2), (2, 2), (4, 3))

    def kernel_gradient(i):
        a = 2 - i
        first, n = chunks[i]
        part = jnp.dot(x_t, hs[2 - a : 6 - a].reshape(256, 256), preferred_element_type=F32)
        parts = [part[:, 0:128], part[:, 128:256]]
        if n == 3:
            parts.append(jnp.dot(x_t, ninths(), preferred_element_type=F32) + loss)
        for v in range(16):
            in_b = jnp.where(c == 0, v % 4, v // 4)
            in_a = jnp.where(c == 0, v // 4, v % 4)
            for k in range(n):
                dw[first + k, in_b, in_a] = parts[k][16 * v : 16 * v + 16].astype(BF16)
        for j in far_first:
            sem = 3 * i + j - 1
            send(
                dw.at[pl.ds(first, n), (pb + j) % 4],
                got_b.at[pl.ds(first, n), j - 1],
                rb_send.at[sem],
                rb_recv.at[sem],
                dev(unit(0, j), c),
            )

    def ninths():
        v = h9[2:6].reshape(256, 128)
        for a in (1, 2):
            v = v + turn(h9[2 - a : 6 - a].reshape(256, 128), a)
        return v.astype(BF16)

    loss = lax.fori_loop(0, 4, frame, jnp.zeros((1, 128), F32))
    loss = jnp.where(group_of((1, 128)) == 3, turn(loss, 3), 0.0)
    kernel_gradient(0)
    for i in (1, 2):
        frame(3 + i, jnp.zeros((1, 128), F32))
        kernel_gradient(i)

    over_last = (((1,), (1,)), ((), ()))
    lat = lax.dot_general(
        ninths(), weights[6].reshape(256, 128), over_last, preferred_element_type=F32
    )
    for a in range(3):
        both = jnp.concatenate(
            [weights[a].reshape(256, 128), weights[3 + a].reshape(256, 128)], axis=1
        )
        lat = lat + lax.dot_general(
            hs[2 - a : 6 - a].reshape(256, 256), both, over_last, preferred_element_type=F32
        )
    lat = lat.reshape(4, 4, 16, 256)
    for i in range(2):
        for core in range(2):
            lat_out[i, core] = lat[2 * i : 2 * i + 2, 2 * core : 2 * core + 2]
    out_own[...] = lat_out[s, c]
    for i, (dz, side, core) in enumerate(((0, s, other), (partner, 1 - s, c), (partner, 1 - s, other))):
        send(
            lat_out.at[side, core],
            out_other.at[i],
            lat_sem.at[i],
            lat_sem.at[3 + i],
            dev(u, core, dz),
        )

    kept = {}

    def axis_a(i):
        first, n = chunks[i]
        part = pl.ds(first, n)
        for j in range(1, 4):
            arrived(got_b.at[part, j - 1], rb_recv.at[3 * i + j - 1])
        for k in far_first + (0,):
            at = (pa + k) % 4
            rows = dw[part, pb, at].astype(F32)
            for j in range(3):
                rows = rows + got_b[part, j, at].astype(F32)
            part_b[part, k] = rows.astype(BF16)
            if k:
                sem = 3 * i + k - 1
                send(
                    part_b.at[part, k],
                    got_a.at[part, k - 1],
                    ra_send.at[sem],
                    ra_recv.at[sem],
                    dev(unit(k, 0), c),
                )

    def swap(i):
        first, n = chunks[i]
        part = pl.ds(first, n)
        rows = part_b[part, 0].astype(F32)
        for j in range(1, 4):
            arrived(got_a.at[part, j - 1], ra_recv.at[3 * i + j - 1])
            rows = rows + got_a[part, j - 1].astype(F32)
        swap_out[part] = jnp.where(c == 0, rows[:, 8:16], rows[:, 0:8])
        kept[i] = jnp.where(c == 0, rows[:, 0:8], rows[:, 8:16])
        send(swap_out.at[part], swap_in.at[part], swap_sem.at[i], swap_sem.at[3 + i], sibling)

    def z_block(p):
        return remote(
            zsend_buf.at[p], zrecv_buf.at[z // 2], z_send.at[p], z_recv.at[z // 2], (2 * p + s, h)
        )

    def along_z(i):
        first, n = chunks[i]
        part = pl.ds(first, n)
        arrived(swap_in.at[part], swap_sem.at[3 + i])
        theirs = swap_in[part]
        zsend_buf[part] = jnp.concatenate(
            [jnp.where(c == 0, kept[i], theirs), jnp.where(c == 0, theirs, kept[i])], axis=1
        ).astype(BF16)
        for p in range(first, first + n):

            @pl.when(z // 2 != p)
            def _():
                z_block(p).start()

    axis_a(0)
    axis_a(1)
    swap(0)
    axis_a(2)
    token_in(2)
    along_z(0)
    swap(1)
    along_z(1)
    swap(2)
    along_z(2)

    def g_copy(i):
        to = (z + i) % Z
        return remote(gsend_buf, grecv_buf.at[z], g_send.at[i], g_recv.at[z], (to, h))

    order = [8] + [v for d in range(7, 0, -1) for v in (d, 16 - d)]

    @pl.when(z < 14)
    def _():
        acc = zsend_buf[z // 2].astype(F32)
        for i in (1, 7, 2, 6, 3, 5, 4):
            source = (z // 2 + i) % 8
            arrived(zrecv_buf.at[source], z_recv.at[source])
            acc = acc + zrecv_buf[source].astype(F32)
        gsend_buf[...] = acc.astype(BF16)
        for i in order:
            g_copy(i).start()
        grecv_buf[z] = gsend_buf[...]

    for i in range(3):
        arrived(out_other.at[i], lat_sem.at[3 + i])
    for copy in sent:
        copy.wait_send()
    @pl.when(s == 0)
    def _():
        for copy in late_copies():
            copy.wait_send()

    for p in range(BLOCKS):

        @pl.when(z // 2 != p)
        def _():
            z_block(p).wait_send()

    def grad_tap(t, pieces, group):
        out_grad[:, t * 128 : (t + 1) * 128] = SCALE * by_group(
            [turn(pieces[q], q - group) for q in range(4)]
        )

    for p in range(BLOCKS):
        pieces = []
        for i in range(2):
            at = 2 * p + i

            @pl.when(z != at)
            def _():
                arrived(grecv_buf.at[at], g_recv.at[at])

            both = grecv_buf[at].astype(F32)
            pieces += [both[0:8], both[8:16]]
        for g in range(4):
            if p < 6:
                grad_tap(9 * (2 - p // 2) + 4 * (p % 2) + g, pieces, g)
            elif g < 3:
                grad_tap(9 * g + 8, pieces, g)
    whole = (pieces[0] + pieces[1] + pieces[2] + pieces[3])[0:1]
    whole = jnp.where(group_of((1, 128)) == 3, whole, 0.0)
    out_loss[0, 0] = jnp.sum(whole) * (1.0 / 16777216)

    @pl.when(z < 14)
    def _():
        for i in order:
            g_copy(i).wait_send()


def per_device(latent, target_frames, master, first_moment, second_moment, ema_weights):
    vmem = pl.BlockSpec(memory_space=pltpu.VMEM)
    hbm = pl.BlockSpec(memory_space=pltpu.HBM)
    dma = pltpu.SemaphoreType.DMA
    quarter_grad = jax.ShapeDtypeStruct(latent.shape, F32)
    grad, own, other, loss = pl.pallas_call(
        kernel,
        out_shape=(
            jax.ShapeDtypeStruct(master.shape, F32),
            quarter_grad,
            jax.ShapeDtypeStruct((3, *latent.shape), F32),
            jax.ShapeDtypeStruct((1, 1), F32),
        ),
        in_specs=[hbm, hbm, hbm],
        out_specs=(vmem, vmem, vmem, pl.BlockSpec(memory_space=pltpu.SMEM)),
        scratch_shapes=[
            pltpu.VMEM((8, 3456), F32),
            pltpu.VMEM((BLOCKS, 8, 128), F32),
            pltpu.VMEM((BLOCKS, 8, 128), F32),
            pltpu.VMEM((BLOCKS, 16, 16, 128), BF16),
            pltpu.VMEM((8, 6, 16, 256), BF16),
            pltpu.VMEM((6, 6, 16, 768), BF16),
            pltpu.VMEM((2, 4, 32, 128), BF16),
            pltpu.VMEM((256, 128), F32),
            pltpu.VMEM((4, 2, 2, 16, 128), BF16),
            pltpu.VMEM((4, 16, 128), BF16),
            pltpu.VMEM((3, 2, 2, 2, 16, 128), BF16),
            pltpu.VMEM((3, 2, 2, 16, 128), BF16),
            pltpu.VMEM((6, 2, 2, 80, 128), F32),
            pltpu.VMEM((6, 96, 384), F32),
            pltpu.VMEM((6, 64, 256), BF16),
            pltpu.VMEM((6, 64, 128), F32),
            pltpu.VMEM((BLOCKS, 4, 4, 16, 128), BF16),
            pltpu.VMEM((BLOCKS, 3, 4, 16, 128), BF16),
            pltpu.VMEM((BLOCKS, 4, 16, 128), BF16),
            pltpu.VMEM((BLOCKS, 3, 16, 128), BF16),
            pltpu.VMEM((BLOCKS, 8, 128), F32),
            pltpu.VMEM((BLOCKS, 8, 128), F32),
            pltpu.VMEM((BLOCKS, 16, 128), BF16),
            pltpu.VMEM((8, 16, 128), BF16),
            pltpu.VMEM((16, 128), BF16),
            pltpu.VMEM((16, 16, 128), BF16),
            pltpu.VMEM((2, 2, 2, 2, 16, 256), F32),
            dma((2,)),
            dma((15,)),
            dma((15,)),
            dma((15,)),
            dma((16,)),
            dma((14,)),
            dma((12,)),
            dma((9,)),
            dma((9,)),
            dma((9,)),
            dma((9,)),
            dma((6,)),
            dma((8,)),
            dma((8,)),
            dma((16,)),
            dma((16,)),
            dma((6,)),
            dma((3,)),
            pltpu.SemaphoreType.REGULAR((3,)),
        ],
        compiler_params=pltpu.CompilerParams(
            collective_id=0, has_side_effects=True, vmem_limit_bytes=40 * 1024 * 1024
        ),
    )(*(pltpu.with_memory_space_constraint(v, pltpu.HBM) for v in (latent, target_frames, master)))
    new_first = beta_first * first_moment + (1.0 - beta_first) * grad
    new_second = beta_second * second_moment + (1.0 - beta_second) * grad * grad
    new_master = master - learn_rate * new_first / (jnp.sqrt(new_second) + adam_eps)
    new_ema = ema_decay * ema_weights + (1.0 - ema_decay) * new_master
    latent_grad = (own + other[0] + other[1] + other[2]).astype(BF16)
    return (new_master, new_first, new_second, new_ema, latent_grad, loss.reshape(()))


def solution(mesh):
    placed = (
        P("tm", "height", None, None),
        P("tm", "height", None, None),
        P("height", None),
        P("height", None),
        P("height", None),
        P("height", None),
    )
    return jax.shard_map(
        per_device,
        mesh=mesh,
        in_specs=placed,
        out_specs=(
            P("height", None),
            P("height", None),
            P("height", None),
            P("height", None),
            P("tm", "height", None, None),
            P(),
        ),
        check_vma=False,
    )
```

```python
import math

import jax
import jax.numpy as jnp
from jax import lax
from jax.experimental import pallas as pl
from jax.experimental.pallas import tpu as pltpu
from jax.sharding import PartitionSpec as P

learn_rate = 0.3
beta_first = 0.9
beta_second = 0.99
ema_decay = 0.9
adam_eps = 1e-08

MESH = pl.DeviceIdType.MESH
F32 = jnp.float32
BF16 = jnp.bfloat16
SCALE = 1.0 / math.sqrt(27 * 256)
BLOCKS = 7
OWNERS = 2
APART = 8 // OWNERS
Z = 16


def group_of(shape):
    return lax.broadcasted_iota(jnp.int32, shape, len(shape) - 1) // 32


def turn(v, groups):
    if isinstance(groups, int) and groups % 4 == 0:
        return v
    return pltpu.roll(v, (groups + 8) % 4 * 32, axis=v.ndim - 1)


def by_group(parts):
    group = group_of(parts[0].shape)
    v = parts[3]
    for i in (2, 1, 0):
        v = jnp.where(group == i, parts[i], v)
    return v


def col_of(shape):
    return lax.broadcasted_iota(jnp.int32, shape, 0) % 16


def from_left(v):
    return jnp.where(col_of(v.shape) == 0, 0.0, pltpu.roll(v, 1, axis=0))


def from_right(v):
    return jnp.where(col_of(v.shape) == 15, 0.0, pltpu.roll(v, v.shape[0] - 1, axis=0))


def quarter_of(m, quarter):
    def tap(a, n, group):
        t = 9 * a + n
        return turn(m[:, t * 128 : (t + 1) * 128], group - quarter)

    blocks = [by_group([tap(a, 4 * k + g, g) for g in range(4)]) for k in range(2) for a in range(3)]
    return blocks + [by_group([tap(g, 8, g) for g in range(3)] + [jnp.zeros((8, 128), F32)])]


def outputs_of(z):
    u = []
    for b in range(3):
        z0, z1, z2 = (turn(z[(3 * b + e) // 4], -((3 * b + e) % 4)) for e in range(3))
        u.append((from_left(z0) + z1 + z2, z0 + z1 + from_right(z2)))
    out = ([], [])
    for j in range(2):
        common = u[0][j][0:80] + u[2][j][16:96]
        out[0].append(common + u[1][j][16:96])
        out[1].append(common + u[1][j][0:80])
    return out


def folded(g):
    slots = []
    for b in range(3):
        v = []
        for j in range(2):
            g0, g1 = g[0][j], g[1][j]
            v.append((g1[16:80] + g0[16:80], g0[0:64] + g1[16:80], g1[0:64] + g0[0:64])[b])
        slots += [v[1] + from_right(v[0]), v[0] + v[1], from_left(v[1]) + v[0]]
    zero = jnp.zeros((64, 128), F32)
    slots += [zero] * 3
    return [by_group([turn(slots[4 * k + g], g) if 4 * k + g < 9 else zero for g in range(4)]) for k in range(3)]


def remote(src, dst, send_sem, recv_sem, device):
    return pltpu.make_async_remote_copy(
        src_ref=src,
        dst_ref=dst,
        send_sem=send_sem,
        recv_sem=recv_sem,
        device_id=device,
        device_id_type=MESH,
    )


def kernel(
    latent,
    target,
    master,
    out_grad,
    out_own,
    out_other,
    out_loss,
    own_kernel,
    pair_out,
    pair_in,
    weights,
    xe,
    xc,
    te,
    tf,
    tpack,
    epack,
    tq,
    eq,
    tp,
    zs,
    hs,
    h9,
    dw,
    got_b,
    part_b,
    got_a,
    swap_out,
    swap_in,
    zsend_buf,
    zrecv_buf,
    gsend_buf,
    grecv_buf,
    lat_out,
    pair_sem,
    ag_send,
    ag_recv,
    x_send,
    x_recv,
    t_send,
    t_recv,
    rb_send,
    rb_recv,
    ra_send,
    ra_recv,
    swap_sem,
    z_send,
    z_recv,
    g_send,
    g_recv,
    lat_sem,
    load_sem,
    token,
):
    z = lax.axis_index("tm")
    h = lax.axis_index("height")
    c = h % 2
    u = h // 2
    s = z % 2
    partner = 1 - 2 * s
    quarter = 2 * s + c
    other = 1 - c
    sa, sb = 4 - 3 * c, 1 + 3 * c
    pa = jnp.where(c == 0, u // 4, u % 4)
    pb = jnp.where(c == 0, u % 4, u // 4)

    def unit(da, db):
        return ((pa + da) % 4) * sa + ((pb + db) % 4) * sb

    def dev(chip, core, dz=0):
        return ((z + dz + Z) % Z, chip * 2 + core)

    sibling = dev(u, other)
    above, below = (u + 15) % 16, (u + 1) % 16
    own_rows = pl.ds(1 + 2 * c, 2)
    own_x = pl.ds(2 + 2 * s, 2)

    loads = [
        pltpu.make_async_copy(src, dst, load_sem.at[i])
        for i, (src, dst) in enumerate(
            ((master, own_kernel), (latent, xe.at[own_x, own_rows]), (target, te))
        )
    ]
    for load in loads:
        load.start()

    barrier = pltpu.get_barrier_semaphore()
    peers = [sibling]
    for j in range(1, 4):
        peers += [dev(unit(j, 0), c), dev(unit(0, j), c)]
    for dz in (-2, -1, 0, 1, 2):
        peers += [dev(above, c, dz), dev(below, c, dz)]
        if dz:
            peers += [dev(u, 0, dz), dev(u, 1, dz)]
    for peer in peers:
        pl.semaphore_signal(barrier, inc=1, device_id=peer, device_id_type=MESH)

    loads[0].wait()
    scaled = own_kernel[...] * SCALE
    for i, block in enumerate(quarter_of(scaled, 2 * s + other)):
        pair_out[i] = block
    mine = quarter_of(scaled, quarter)

    pl.semaphore_wait(barrier, len(peers))

    sent = []

    def send(*args):
        copy = remote(*args)
        copy.start()
        sent.append(copy)

    def arrived(dst, sem):
        remote(dst, dst, ag_send.at[0], sem, sibling).wait_recv()

    def token_out(i):
        for step in (1 << i, -(1 << i)):
            pl.semaphore_signal(
                token.at[i], inc=1, device_id=dev(u, c, step), device_id_type=MESH
            )

    def token_in(i):
        pl.semaphore_wait(token.at[i], 2)

    token_out(0)
    send(pair_out, pair_in, pair_sem.at[0], pair_sem.at[1], sibling)

    edge = pl.ds(c, 1)
    edge_to = jnp.where(c == 0, above, below)
    edge_row = pl.ds(5 - 5 * c, 1)
    beside = 2 * s - 1
    routes = ((0, 1 + s), (partner, 1 + s), (beside, 3 - 3 * s), (2 * beside, 3 - 3 * s))

    def send_latent():
        n = 0
        for i, (dz, t) in enumerate(routes):
            send(
                latent,
                xe.at[pl.ds(2 * t, 2), own_rows],
                x_send.at[n],
                x_recv.at[2 * t + c],
                dev(u, c if i else other, dz),
            )
            n += 1
        for dz, t in routes:
            send(
                latent.at[:, edge],
                xe.at[pl.ds(2 * t, 2), edge_row],
                x_send.at[n],
                x_recv.at[8 + 2 * t + c],
                dev(edge_to, c, dz),
            )
            n += 1

    def pack_target():
        tf[...] = te[...].astype(F32).reshape(256, 128)
        edges = []
        for f in range(2):
            for j in range(2):
                rows = [tf[pl.ds((4 * f + r) * 32 + j, 16, stride=2), :] for r in range(4)]
                for q in range(4):
                    tpack[q, f, j] = by_group([turn(rows[r], r - q) for r in range(4)]).astype(BF16)
                edges.append(jnp.where(c == 0, rows[0], rows[3]))
        for q in range(4):
            epack[q] = by_group([turn(edges[g], g - q) for g in range(4)]).astype(BF16)
        tq[s, c] = tpack[quarter]

    def target_copies(first, steps, slot):
        copies = []

        def add(src, dst, recv_sem, device):
            copies.append(remote(src, dst, t_send.at[first + len(copies)], recv_sem, device))

        for dz, side in steps:
            near = isinstance(dz, int) and dz == 0
            for core in (other,) if near else (c, other):
                add(tpack.at[2 * side + core], tq.at[slot, c], t_recv.at[2 * slot + c], dev(u, core, dz))
            add(
                epack.at[pl.ds(2 * side, 2)],
                eq.at[slot, c],
                t_recv.at[6 + 2 * slot + c],
                dev(edge_to, c, dz),
            )
        return copies

    def late_copies():
        return target_copies(5, ((-1, 1), (-2, 0)), 2)

    def send_target():
        for copy in target_copies(0, ((0, s), (partner, 1 - s)), s):
            copy.start()
            sent.append(copy)

        @pl.when(s == 0)
        def _():
            for copy in late_copies():
                copy.start()

    loads[2].wait()
    pack_target()

    arrived(pair_in, pair_sem.at[1])
    for i in range(BLOCKS):
        theirs = pair_in[i]
        rows = jnp.concatenate(
            [jnp.where(c == 0, mine[i], theirs), jnp.where(c == 0, theirs, mine[i])], axis=0
        )
        weights[i, u] = rows.astype(BF16)

    def send_unit(index, sem, to):
        place = weights.at[:, index]
        send(place, place, ag_send.at[sem], ag_recv.at[sem], dev(to, c))

    far_first = (2, 1, 3)
    for j in far_first:
        send_unit(u, j - 1, unit(j, 0))
    for j in far_first:
        send_unit(u, 2 + j, unit(0, j))
    send_latent()
    send_target()
    for k in (1, 3, 2):
        index = unit(4 - k, 0)
        arrived(weights.at[:, index], ag_recv.at[k - 1])
        for j in far_first:
            send_unit(index, 2 + 3 * k + j, unit(0, j))
    token_in(0)
    token_out(1)

    def hand_on(place, send_sem, recv_sem):
        arrived(place, recv_sem)
        send(place, place, send_sem, recv_sem, sibling)

    for n, t in enumerate((2 - s, 3, 0)):
        hand_on(xe.at[pl.ds(2 * t, 2), own_rows], x_send.at[12 + n], x_recv.at[2 * t + c])
    for t in range(4):
        hand_on(xe.at[pl.ds(2 * t, 2), edge_row], x_send.at[8 + t], x_recv.at[8 + 2 * t + c])
    for t in range(3):
        recv_sem = t_recv.at[6 + 2 * t + c]
        arrived(eq.at[t, c], recv_sem)
        place = eq.at[t, c, other]
        send(place, place, t_send.at[11 + t], recv_sem, sibling)

    loads[1].wait()
    for t in range(4):
        arrived(xe.at[pl.ds(2 * t, 2), pl.ds(1 + 2 * other, 2)], x_recv.at[2 * t + other])
        arrived(xe.at[pl.ds(2 * t, 2), pl.ds(5 - 5 * other, 1)], x_recv.at[8 + 2 * t + other])

    for a in range(3):
        xc[:, :, :, a * 256 : (a + 1) * 256] = xe[a : a + 6]

    @pl.when(u == 0)
    def _():
        xc[:, 0] = jnp.zeros((6, 16, 768), BF16)

    @pl.when(u == 15)
    def _():
        xc[:, 5] = jnp.zeros((6, 16, 768), BF16)

    @pl.when(z < 2)
    def _():
        xc[0:2, :, :, 0:256] = jnp.zeros((2, 6, 16, 256), BF16)
        xc[0:1, :, :, 256:512] = jnp.zeros((1, 6, 16, 256), BF16)

    x_t = xe[2:6, 1:5].reshape(256, 256).astype(F32).T.astype(BF16)

    for t, core in ((1 - s, c), (2, c), (0, other), (1, other), (2, other)):
        arrived(tq.at[t, core], t_recv.at[2 * t + core])
    for t in range(3):
        arrived(eq.at[t, other, c], t_recv.at[6 + 2 * t + other])

    for t in range(3):
        edges = [eq[t, core, c].astype(F32) for core in range(2)]
        for f in range(2):
            for j in range(2):
                at = 2 * t + f
                tp[at, 0, j, 64:80] = turn(edges[0], -(2 * f + j))
                tp[at, 1, j, 0:16] = turn(edges[1], -(2 * f + j))
                for core in range(2):
                    rows = tq[t, core, f, j].astype(F32)
                    for r in range(2):
                        for i in range(2):
                            k = 16 * (2 * core + r + i)
                            tp[at, i, j, k : k + 16] = turn(rows, -(2 * r + i))
    token_in(1)
    token_out(2)

    for k in (0, 3, 1, 2):
        for j in far_first:
            arrived(weights.at[:, unit(4 - k, 4 - j)], ag_recv.at[2 + 3 * k + j])

    ninth = weights[6].reshape(256, 128).astype(F32)
    by_slot = jnp.concatenate(
        [
            weights[0:3].reshape(768, 128),
            weights[3:6].reshape(768, 128),
            jnp.concatenate([turn(ninth, -a).astype(BF16) for a in range(3)], axis=0),
        ],
        axis=1,
    )
    zs[...] = jnp.dot(
        xc[...].reshape(576, 768), by_slot, preferred_element_type=F32
    ).reshape(6, 96, 384)

    def frame(f, loss):
        out = outputs_of([zs[f, :, k * 128 : (k + 1) * 128] for k in range(3)])
        row = lax.broadcasted_iota(jnp.int32, (80, 128), 0)
        keep = jnp.logical_or(f < 4, z < Z - 2)
        keep0 = jnp.logical_and(keep, jnp.logical_or(row < 64, u < 15))
        keep1 = jnp.logical_and(keep, jnp.logical_or(row >= 16, u > 0))
        own = jnp.where(f < 4, 1.0, 0.0)
        g = ([], [])
        for i in range(2):
            for j in range(2):
                misfit = out[i][j] - tp[f, i, j]
                counted = misfit[16 * i : 16 * i + 64]
                loss = loss + own * jnp.sum(counted * counted, axis=0, keepdims=True)
                rounded = misfit.astype(BF16).astype(F32)
                g[i].append(jnp.where((keep0, keep1)[i], rounded, 0.0))
        blocks = folded(g)
        for k in range(2):
            hs[f, :, k * 128 : (k + 1) * 128] = blocks[k].astype(BF16)
        h9[f] = blocks[2]
        return loss

    chunks = ((0, 2), (2, 2), (4, 3))

    def kernel_gradient(i):
        a = 2 - i
        first, n = chunks[i]
        part = jnp.dot(x_t, hs[2 - a : 6 - a].reshape(256, 256), preferred_element_type=F32)
        parts = [part[:, 0:128], part[:, 128:256]]
        if n == 3:
            parts.append(jnp.dot(x_t, ninths(), preferred_element_type=F32) + loss)
        for v in range(16):
            in_b = jnp.where(c == 0, v % 4, v // 4)
            in_a = jnp.where(c == 0, v // 4, v % 4)
            for k in range(n):
                dw[first + k, in_b, in_a] = parts[k][16 * v : 16 * v + 16].astype(BF16)
        for j in far_first:
            sem = 3 * i + j - 1
            send(
                dw.at[pl.ds(first, n), (pb + j) % 4],
                got_b.at[pl.ds(first, n), j - 1],
                rb_send.at[sem],
                rb_recv.at[sem],
                dev(unit(0, j), c),
            )

    def ninths():
        v = h9[2:6].reshape(256, 128)
        for a in (1, 2):
            v = v + turn(h9[2 - a : 6 - a].reshape(256, 128), a)
        return v.astype(BF16)

    loss = lax.fori_loop(0, 4, frame, jnp.zeros((1, 128), F32))
    loss = jnp.where(group_of((1, 128)) == 3, turn(loss, 3), 0.0)
    kernel_gradient(0)
    for i in (1, 2):
        frame(3 + i, jnp.zeros((1, 128), F32))
        kernel_gradient(i)

    over_last = (((1,), (1,)), ((), ()))
    lat = lax.dot_general(
        ninths(), weights[6].reshape(256, 128), over_last, preferred_element_type=F32
    )
    for a in range(3):
        both = jnp.concatenate(
            [weights[a].reshape(256, 128), weights[3 + a].reshape(256, 128)], axis=1
        )
        lat = lat + lax.dot_general(
            hs[2 - a : 6 - a].reshape(256, 256), both, over_last, preferred_element_type=F32
        )
    lat = lat.reshape(4, 4, 16, 256)
    for i in range(2):
        for core in range(2):
            lat_out[i, core] = lat[2 * i : 2 * i + 2, 2 * core : 2 * core + 2]
    out_own[...] = lat_out[s, c]
    for i, (dz, side, core) in enumerate(((0, s, other), (partner, 1 - s, c), (partner, 1 - s, other))):
        send(
            lat_out.at[side, core],
            out_other.at[i],
            lat_sem.at[i],
            lat_sem.at[3 + i],
            dev(u, core, dz),
        )

    kept = {}

    def axis_a(i):
        first, n = chunks[i]
        part = pl.ds(first, n)
        for j in range(1, 4):
            arrived(got_b.at[part, j - 1], rb_recv.at[3 * i + j - 1])
        for k in far_first + (0,):
            at = (pa + k) % 4
            rows = dw[part, pb, at].astype(F32)
            for j in range(3):
                rows = rows + got_b[part, j, at].astype(F32)
            part_b[part, k] = rows.astype(BF16)
            if k:
                sem = 3 * i + k - 1
                send(
                    part_b.at[part, k],
                    got_a.at[part, k - 1],
                    ra_send.at[sem],
                    ra_recv.at[sem],
                    dev(unit(k, 0), c),
                )

    def swap(i):
        first, n = chunks[i]
        part = pl.ds(first, n)
        rows = part_b[part, 0].astype(F32)
        for j in range(1, 4):
            arrived(got_a.at[part, j - 1], ra_recv.at[3 * i + j - 1])
            rows = rows + got_a[part, j - 1].astype(F32)
        swap_out[part] = jnp.where(c == 0, rows[:, 8:16], rows[:, 0:8])
        kept[i] = jnp.where(c == 0, rows[:, 0:8], rows[:, 8:16])
        send(swap_out.at[part], swap_in.at[part], swap_sem.at[i], swap_sem.at[3 + i], sibling)

    mine_at = z // 2

    def z_block(p, slot):
        owner = (p - APART * slot) % 8
        return remote(
            zsend_buf.at[p],
            zrecv_buf.at[slot, mine_at],
            z_send.at[OWNERS * p + slot],
            z_recv.at[8 * slot + mine_at],
            (2 * owner + s, h),
        )

    def along_z(i):
        first, n = chunks[i]
        part = pl.ds(first, n)
        arrived(swap_in.at[part], swap_sem.at[3 + i])
        theirs = swap_in[part]
        zsend_buf[part] = jnp.concatenate(
            [jnp.where(c == 0, kept[i], theirs), jnp.where(c == 0, theirs, kept[i])], axis=1
        ).astype(BF16)
        for p in range(first, first + n):

            for slot in range(OWNERS):

                @pl.when(mine_at != (p - APART * slot) % 8)
                def _():
                    z_block(p, slot).start()

    axis_a(0)
    axis_a(1)
    swap(0)
    axis_a(2)
    token_in(2)
    along_z(0)
    swap(1)
    along_z(1)
    swap(2)
    along_z(2)

    def g_copy(slot, step):
        block = 2 * ((mine_at + APART * slot) % 8) + s
        n = (2 * APART - 1) * slot + (step + APART if step < 0 else step + APART - 1)
        return remote(
            gsend_buf.at[slot], grecv_buf.at[block], g_send.at[n], g_recv.at[block], ((z + step + Z) % Z, h)
        )

    steps = [v for d in range(APART, 0, -1) for v in (-d, d - 1) if v]

    for j in range(OWNERS):
        slot = (j - mine_at // APART + OWNERS) % OWNERS
        block = mine_at % APART + APART * j

        @pl.when(block < BLOCKS)
        def _():
            zrecv_buf[slot, mine_at] = zsend_buf[block]
            for i in (1, 7, 2, 6, 3, 5, 4):
                source = (mine_at + i) % 8
                arrived(zrecv_buf.at[slot, source], z_recv.at[8 * slot + source])
            acc = zrecv_buf[slot, 0].astype(F32)
            for i in range(1, 8):
                acc = acc + zrecv_buf[slot, i].astype(F32)
            gsend_buf[slot] = acc.astype(BF16)
            for step in steps:
                g_copy(slot, step).start()
            grecv_buf[2 * block + s] = gsend_buf[slot]

    for i in range(3):
        arrived(out_other.at[i], lat_sem.at[3 + i])
    for copy in sent:
        copy.wait_send()
    @pl.when(s == 0)
    def _():
        for copy in late_copies():
            copy.wait_send()

    for p in range(BLOCKS):

        for slot in range(OWNERS):

            @pl.when(mine_at != (p - APART * slot) % 8)
            def _():
                z_block(p, slot).wait_send()

    for slot in range(OWNERS):

        @pl.when((mine_at + APART * slot) % 8 < BLOCKS)
        def _():
            for step in steps:
                g_copy(slot, step).wait_send()

    def grad_tap(t, pieces, group):
        out_grad[:, t * 128 : (t + 1) * 128] = SCALE * by_group(
            [turn(pieces[q], q - group) for q in range(4)]
        )

    for p in range(BLOCKS):
        pieces = []
        for i in range(2):
            at = 2 * p + i

            @pl.when((z - at + Z) % (2 * APART) != 0)
            def _():
                arrived(grecv_buf.at[at], g_recv.at[at])

            both = grecv_buf[at].astype(F32)
            pieces += [both[0:8], both[8:16]]
        for g in range(4):
            if p < 6:
                grad_tap(9 * (2 - p // 2) + 4 * (p % 2) + g, pieces, g)
            elif g < 3:
                grad_tap(9 * g + 8, pieces, g)
    whole = (pieces[0] + pieces[1] + pieces[2] + pieces[3])[0:1]
    whole = jnp.where(group_of((1, 128)) == 3, whole, 0.0)
    out_loss[0, 0] = jnp.sum(whole) * (1.0 / 16777216)


def per_device(latent, target_frames, master, first_moment, second_moment, ema_weights):
    vmem = pl.BlockSpec(memory_space=pltpu.VMEM)
    hbm = pl.BlockSpec(memory_space=pltpu.HBM)
    dma = pltpu.SemaphoreType.DMA
    quarter_grad = jax.ShapeDtypeStruct(latent.shape, F32)
    grad, own, other, loss = pl.pallas_call(
        kernel,
        out_shape=(
            jax.ShapeDtypeStruct(master.shape, F32),
            quarter_grad,
            jax.ShapeDtypeStruct((3, *latent.shape), F32),
            jax.ShapeDtypeStruct((1, 1), F32),
        ),
        in_specs=[hbm, hbm, hbm],
        out_specs=(vmem, vmem, vmem, pl.BlockSpec(memory_space=pltpu.SMEM)),
        scratch_shapes=[
            pltpu.VMEM((8, 3456), F32),
            pltpu.VMEM((BLOCKS, 8, 128), F32),
            pltpu.VMEM((BLOCKS, 8, 128), F32),
            pltpu.VMEM((BLOCKS, 16, 16, 128), BF16),
            pltpu.VMEM((8, 6, 16, 256), BF16),
            pltpu.VMEM((6, 6, 16, 768), BF16),
            pltpu.VMEM((2, 4, 32, 128), BF16),
            pltpu.VMEM((256, 128), F32),
            pltpu.VMEM((4, 2, 2, 16, 128), BF16),
            pltpu.VMEM((4, 16, 128), BF16),
            pltpu.VMEM((3, 2, 2, 2, 16, 128), BF16),
            pltpu.VMEM((3, 2, 2, 16, 128), BF16),
            pltpu.VMEM((6, 2, 2, 80, 128), F32),
            pltpu.VMEM((6, 96, 384), F32),
            pltpu.VMEM((6, 64, 256), BF16),
            pltpu.VMEM((6, 64, 128), F32),
            pltpu.VMEM((BLOCKS, 4, 4, 16, 128), BF16),
            pltpu.VMEM((BLOCKS, 3, 4, 16, 128), BF16),
            pltpu.VMEM((BLOCKS, 4, 16, 128), BF16),
            pltpu.VMEM((BLOCKS, 3, 16, 128), BF16),
            pltpu.VMEM((BLOCKS, 8, 128), F32),
            pltpu.VMEM((BLOCKS, 8, 128), F32),
            pltpu.VMEM((BLOCKS, 16, 128), BF16),
            pltpu.VMEM((OWNERS, 8, 16, 128), BF16),
            pltpu.VMEM((OWNERS, 16, 128), BF16),
            pltpu.VMEM((16, 16, 128), BF16),
            pltpu.VMEM((2, 2, 2, 2, 16, 256), F32),
            dma((2,)),
            dma((15,)),
            dma((15,)),
            dma((15,)),
            dma((16,)),
            dma((14,)),
            dma((12,)),
            dma((9,)),
            dma((9,)),
            dma((9,)),
            dma((9,)),
            dma((6,)),
            dma((OWNERS * BLOCKS,)),
            dma((OWNERS * 8,)),
            dma((16,)),
            dma((16,)),
            dma((6,)),
            dma((3,)),
            pltpu.SemaphoreType.REGULAR((3,)),
        ],
        compiler_params=pltpu.CompilerParams(
            collective_id=0, has_side_effects=True, vmem_limit_bytes=40 * 1024 * 1024
        ),
    )(*(pltpu.with_memory_space_constraint(v, pltpu.HBM) for v in (latent, target_frames, master)))
    new_first = beta_first * first_moment + (1.0 - beta_first) * grad
    new_second = beta_second * second_moment + (1.0 - beta_second) * grad * grad
    new_master = master - learn_rate * new_first / (jnp.sqrt(new_second) + adam_eps)
    new_ema = ema_decay * ema_weights + (1.0 - ema_decay) * new_master
    latent_grad = (own + other[0] + other[1] + other[2]).astype(BF16)
    return (new_master, new_first, new_second, new_ema, latent_grad, loss.reshape(()))


def solution(mesh):
    placed = (
        P("tm", "height", None, None),
        P("tm", "height", None, None),
        P("height", None),
        P("height", None),
        P("height", None),
        P("height", None),
    )
    return jax.shard_map(
        per_device,
        mesh=mesh,
        in_specs=placed,
        out_specs=(
            P("height", None),
            P("height", None),
            P("height", None),
            P("height", None),
            P("tm", "height", None, None),
            P(),
        ),
        check_vma=False,
    )
```

```python
import math

import jax
import jax.numpy as jnp
from jax import lax
from jax.experimental import pallas as pl
from jax.experimental.pallas import tpu as pltpu
from jax.sharding import PartitionSpec as P

learn_rate = 0.3
beta_first = 0.9
beta_second = 0.99
ema_decay = 0.9
adam_eps = 1e-08

MESH = pl.DeviceIdType.MESH
F32 = jnp.float32
BF16 = jnp.bfloat16
SCALE = 1.0 / math.sqrt(27 * 256)
BLOCKS = 7
OWNERS = 2
APART = 8 // OWNERS
Z = 16


def group_of(shape):
    return lax.broadcasted_iota(jnp.int32, shape, len(shape) - 1) // 32


def turn(v, groups):
    if isinstance(groups, int) and groups % 4 == 0:
        return v
    return pltpu.roll(v, (groups + 8) % 4 * 32, axis=v.ndim - 1)


def by_group(parts):
    group = group_of(parts[0].shape)
    v = parts[3]
    for i in (2, 1, 0):
        v = jnp.where(group == i, parts[i], v)
    return v


def col_of(shape):
    return lax.broadcasted_iota(jnp.int32, shape, 0) % 16


def from_left(v):
    return jnp.where(col_of(v.shape) == 0, 0.0, pltpu.roll(v, 1, axis=0))


def from_right(v):
    return jnp.where(col_of(v.shape) == 15, 0.0, pltpu.roll(v, v.shape[0] - 1, axis=0))


def quarter_of(m, quarter):
    def tap(a, n, group):
        t = 9 * a + n
        return turn(m[:, t * 128 : (t + 1) * 128], group - quarter)

    blocks = [by_group([tap(a, 4 * k + g, g) for g in range(4)]) for k in range(2) for a in range(3)]
    return blocks + [by_group([tap(g, 8, g) for g in range(3)] + [jnp.zeros((8, 128), F32)])]


def outputs_of(z):
    u = []
    for b in range(3):
        z0, z1, z2 = (turn(z[(3 * b + e) // 4], -((3 * b + e) % 4)) for e in range(3))
        u.append((from_left(z0) + z1 + z2, z0 + z1 + from_right(z2)))
    out = ([], [])
    for j in range(2):
        common = u[0][j][0:80] + u[2][j][16:96]
        out[0].append(common + u[1][j][16:96])
        out[1].append(common + u[1][j][0:80])
    return out


def folded(g):
    slots = []
    for b in range(3):
        v = []
        for j in range(2):
            g0, g1 = g[0][j], g[1][j]
            v.append((g1[16:80] + g0[16:80], g0[0:64] + g1[16:80], g1[0:64] + g0[0:64])[b])
        slots += [v[1] + from_right(v[0]), v[0] + v[1], from_left(v[1]) + v[0]]
    zero = jnp.zeros((64, 128), F32)
    slots += [zero] * 3
    return [by_group([turn(slots[4 * k + g], g) if 4 * k + g < 9 else zero for g in range(4)]) for k in range(3)]


def remote(src, dst, send_sem, recv_sem, device):
    return pltpu.make_async_remote_copy(
        src_ref=src,
        dst_ref=dst,
        send_sem=send_sem,
        recv_sem=recv_sem,
        device_id=device,
        device_id_type=MESH,
    )


def kernel(
    latent,
    target,
    master,
    out_grad,
    out_own,
    out_other,
    out_loss,
    own_kernel,
    pair_out,
    pair_in,
    weights,
    xe,
    xc,
    te,
    tf,
    tpack,
    epack,
    tq,
    eq,
    tp,
    zs,
    hs,
    h9,
    dw,
    got_b,
    part_b,
    got_a,
    swap_out,
    swap_in,
    zsend_buf,
    zrecv_buf,
    gsend_buf,
    grecv_buf,
    lat_out,
    pair_sem,
    ag_send,
    ag_recv,
    x_send,
    x_recv,
    t_send,
    t_recv,
    rb_send,
    rb_recv,
    ra_send,
    ra_recv,
    swap_sem,
    z_send,
    z_recv,
    g_send,
    g_recv,
    lat_sem,
    load_sem,
    token,
):
    z = lax.axis_index("tm")
    h = lax.axis_index("height")
    c = h % 2
    u = h // 2
    s = z % 2
    partner = 1 - 2 * s
    quarter = 2 * s + c
    other = 1 - c
    sa, sb = 4 - 3 * c, 1 + 3 * c
    pa = jnp.where(c == 0, u // 4, u % 4)
    pb = jnp.where(c == 0, u % 4, u // 4)

    def unit(da, db):
        return ((pa + da) % 4) * sa + ((pb + db) % 4) * sb

    def dev(chip, core, dz=0):
        return ((z + dz + Z) % Z, chip * 2 + core)

    sibling = dev(u, other)
    above, below = (u + 15) % 16, (u + 1) % 16
    own_rows = pl.ds(1 + 2 * c, 2)
    own_x = pl.ds(2 + 2 * s, 2)

    loads = [
        pltpu.make_async_copy(src, dst, load_sem.at[i])
        for i, (src, dst) in enumerate(
            ((master, own_kernel), (latent, xe.at[own_x, own_rows]), (target, te))
        )
    ]
    for load in loads:
        load.start()

    barrier = pltpu.get_barrier_semaphore()
    peers = [sibling]
    for j in range(1, 4):
        peers += [dev(unit(j, 0), c), dev(unit(0, j), c)]
    for dz in (-2, -1, 0, 1, 2):
        peers += [dev(above, c, dz), dev(below, c, dz)]
        if dz:
            peers += [dev(u, 0, dz), dev(u, 1, dz)]
    for peer in peers:
        pl.semaphore_signal(barrier, inc=1, device_id=peer, device_id_type=MESH)

    loads[0].wait()
    scaled = own_kernel[...] * SCALE
    for i, block in enumerate(quarter_of(scaled, 2 * s + other)):
        pair_out[i] = block
    mine = quarter_of(scaled, quarter)

    pl.semaphore_wait(barrier, len(peers))

    sent = []

    def send(*args):
        copy = remote(*args)
        copy.start()
        sent.append(copy)

    def arrived(dst, sem):
        remote(dst, dst, ag_send.at[0], sem, sibling).wait_recv()

    def token_out(i):
        for step in (1 << i, -(1 << i)):
            pl.semaphore_signal(
                token.at[i], inc=1, device_id=dev(u, c, step), device_id_type=MESH
            )

    def token_in(i):
        pl.semaphore_wait(token.at[i], 2)

    token_out(0)
    send(pair_out, pair_in, pair_sem.at[0], pair_sem.at[1], sibling)

    edge = pl.ds(c, 1)
    edge_to = jnp.where(c == 0, above, below)
    edge_row = pl.ds(5 - 5 * c, 1)
    beside = 2 * s - 1
    routes = ((0, 1 + s), (partner, 1 + s), (beside, 3 - 3 * s), (2 * beside, 3 - 3 * s))

    def send_latent():
        n = 0
        for i, (dz, t) in enumerate(routes):
            send(
                latent,
                xe.at[pl.ds(2 * t, 2), own_rows],
                x_send.at[n],
                x_recv.at[2 * t + c],
                dev(u, c if i else other, dz),
            )
            n += 1
        for dz, t in routes:
            send(
                latent.at[:, edge],
                xe.at[pl.ds(2 * t, 2), edge_row],
                x_send.at[n],
                x_recv.at[8 + 2 * t + c],
                dev(edge_to, c, dz),
            )
            n += 1

    def pack_target():
        tf[...] = te[...].astype(F32).reshape(256, 128)
        edges = []
        for f in range(2):
            for j in range(2):
                rows = [tf[pl.ds((4 * f + r) * 32 + j, 16, stride=2), :] for r in range(4)]
                for q in range(4):
                    tpack[q, f, j] = by_group([turn(rows[r], r - q) for r in range(4)]).astype(BF16)
                edges.append(jnp.where(c == 0, rows[0], rows[3]))
        for q in range(4):
            epack[q] = by_group([turn(edges[g], g - q) for g in range(4)]).astype(BF16)
        tq[s, c] = tpack[quarter]

    def target_copies(first, steps, slot):
        copies = []

        def add(src, dst, recv_sem, device):
            copies.append(remote(src, dst, t_send.at[first + len(copies)], recv_sem, device))

        for dz, side in steps:
            near = isinstance(dz, int) and dz == 0
            for core in (other,) if near else (c, other):
                add(tpack.at[2 * side + core], tq.at[slot, c], t_recv.at[2 * slot + c], dev(u, core, dz))
            add(
                epack.at[pl.ds(2 * side, 2)],
                eq.at[slot, c],
                t_recv.at[6 + 2 * slot + c],
                dev(edge_to, c, dz),
            )
        return copies

    def late_copies():
        return target_copies(5, ((-1, 1), (-2, 0)), 2)

    def send_target():
        for copy in target_copies(0, ((0, s), (partner, 1 - s)), s):
            copy.start()
            sent.append(copy)

        @pl.when(s == 0)
        def _():
            for copy in late_copies():
                copy.start()

    send_latent()
    loads[2].wait()
    pack_target()

    arrived(pair_in, pair_sem.at[1])
    for i in range(BLOCKS):
        theirs = pair_in[i]
        rows = jnp.concatenate(
            [jnp.where(c == 0, mine[i], theirs), jnp.where(c == 0, theirs, mine[i])], axis=0
        )
        weights[i, u] = rows.astype(BF16)

    def send_unit(index, sem, to):
        place = weights.at[:, index]
        send(place, place, ag_send.at[sem], ag_recv.at[sem], dev(to, c))

    far_first = (2, 1, 3)
    for j in far_first:
        send_unit(u, j - 1, unit(j, 0))
    for j in far_first:
        send_unit(u, 2 + j, unit(0, j))
    send_target()
    for k in (1, 3, 2):
        index = unit(4 - k, 0)
        arrived(weights.at[:, index], ag_recv.at[k - 1])
        for j in far_first:
            send_unit(index, 2 + 3 * k + j, unit(0, j))
    token_in(0)
    token_out(1)

    def hand_on(place, send_sem, recv_sem):
        arrived(place, recv_sem)
        send(place, place, send_sem, recv_sem, sibling)

    for n, t in enumerate((2 - s, 3, 0)):
        hand_on(xe.at[pl.ds(2 * t, 2), own_rows], x_send.at[12 + n], x_recv.at[2 * t + c])
    for t in range(4):
        hand_on(xe.at[pl.ds(2 * t, 2), edge_row], x_send.at[8 + t], x_recv.at[8 + 2 * t + c])
    for t in range(3):
        recv_sem = t_recv.at[6 + 2 * t + c]
        arrived(eq.at[t, c], recv_sem)
        place = eq.at[t, c, other]
        send(place, place, t_send.at[11 + t], recv_sem, sibling)

    loads[1].wait()
    for t in range(4):
        arrived(xe.at[pl.ds(2 * t, 2), pl.ds(1 + 2 * other, 2)], x_recv.at[2 * t + other])
        arrived(xe.at[pl.ds(2 * t, 2), pl.ds(5 - 5 * other, 1)], x_recv.at[8 + 2 * t + other])

    for a in range(3):
        xc[:, :, :, a * 256 : (a + 1) * 256] = xe[a : a + 6]

    @pl.when(u == 0)
    def _():
        xc[:, 0] = jnp.zeros((6, 16, 768), BF16)

    @pl.when(u == 15)
    def _():
        xc[:, 5] = jnp.zeros((6, 16, 768), BF16)

    @pl.when(z < 2)
    def _():
        xc[0:2, :, :, 0:256] = jnp.zeros((2, 6, 16, 256), BF16)
        xc[0:1, :, :, 256:512] = jnp.zeros((1, 6, 16, 256), BF16)

    x_t = xe[2:6, 1:5].reshape(256, 256).astype(F32).T.astype(BF16)

    for t, core in ((1 - s, c), (2, c), (0, other), (1, other), (2, other)):
        arrived(tq.at[t, core], t_recv.at[2 * t + core])
    for t in range(3):
        arrived(eq.at[t, other, c], t_recv.at[6 + 2 * t + other])

    for t in range(3):
        edges = [eq[t, core, c].astype(F32) for core in range(2)]
        for f in range(2):
            for j in range(2):
                at = 2 * t + f
                tp[at, 0, j, 64:80] = turn(edges[0], -(2 * f + j))
                tp[at, 1, j, 0:16] = turn(edges[1], -(2 * f + j))
                for core in range(2):
                    rows = tq[t, core, f, j].astype(F32)
                    for r in range(2):
                        for i in range(2):
                            k = 16 * (2 * core + r + i)
                            tp[at, i, j, k : k + 16] = turn(rows, -(2 * r + i))
    token_in(1)
    token_out(2)

    for k in (0, 3, 1, 2):
        for j in far_first:
            arrived(weights.at[:, unit(4 - k, 4 - j)], ag_recv.at[2 + 3 * k + j])

    ninth = weights[6].reshape(256, 128).astype(F32)
    by_slot = jnp.concatenate(
        [
            weights[0:3].reshape(768, 128),
            weights[3:6].reshape(768, 128),
            jnp.concatenate([turn(ninth, -a).astype(BF16) for a in range(3)], axis=0),
        ],
        axis=1,
    )
    zs[...] = jnp.dot(
        xc[...].reshape(576, 768), by_slot, preferred_element_type=F32
    ).reshape(6, 96, 384)

    def frame(f, loss):
        out = outputs_of([zs[f, :, k * 128 : (k + 1) * 128] for k in range(3)])
        row = lax.broadcasted_iota(jnp.int32, (80, 128), 0)
        keep = jnp.logical_or(f < 4, z < Z - 2)
        keep0 = jnp.logical_and(keep, jnp.logical_or(row < 64, u < 15))
        keep1 = jnp.logical_and(keep, jnp.logical_or(row >= 16, u > 0))
        own = jnp.where(f < 4, 1.0, 0.0)
        g = ([], [])
        for i in range(2):
            for j in range(2):
                misfit = out[i][j] - tp[f, i, j]
                counted = misfit[16 * i : 16 * i + 64]
                loss = loss + own * jnp.sum(counted * counted, axis=0, keepdims=True)
                rounded = misfit.astype(BF16).astype(F32)
                g[i].append(jnp.where((keep0, keep1)[i], rounded, 0.0))
        blocks = folded(g)
        for k in range(2):
            hs[f, :, k * 128 : (k + 1) * 128] = blocks[k].astype(BF16)
        h9[f] = blocks[2]
        return loss

    chunks = ((0, 2), (2, 2), (4, 3))

    def kernel_gradient(i):
        a = 2 - i
        first, n = chunks[i]
        part = jnp.dot(x_t, hs[2 - a : 6 - a].reshape(256, 256), preferred_element_type=F32)
        parts = [part[:, 0:128], part[:, 128:256]]
        if n == 3:
            parts.append(jnp.dot(x_t, ninths(), preferred_element_type=F32) + loss)
        for v in range(16):
            in_b = jnp.where(c == 0, v % 4, v // 4)
            in_a = jnp.where(c == 0, v // 4, v % 4)
            for k in range(n):
                dw[first + k, in_b, in_a] = parts[k][16 * v : 16 * v + 16].astype(BF16)
        for j in far_first:
            sem = 3 * i + j - 1
            send(
                dw.at[pl.ds(first, n), (pb + j) % 4],
                got_b.at[pl.ds(first, n), j - 1],
                rb_send.at[sem],
                rb_recv.at[sem],
                dev(unit(0, j), c),
            )

    def ninths():
        v = h9[2:6].reshape(256, 128)
        for a in (1, 2):
            v = v + turn(h9[2 - a : 6 - a].reshape(256, 128), a)
        return v.astype(BF16)

    loss = lax.fori_loop(0, 4, frame, jnp.zeros((1, 128), F32))
    loss = jnp.where(group_of((1, 128)) == 3, turn(loss, 3), 0.0)
    kernel_gradient(0)
    for i in (1, 2):
        frame(3 + i, jnp.zeros((1, 128), F32))
        kernel_gradient(i)

    over_last = (((1,), (1,)), ((), ()))
    lat = lax.dot_general(
        ninths(), weights[6].reshape(256, 128), over_last, preferred_element_type=F32
    )
    for a in range(3):
        both = jnp.concatenate(
            [weights[a].reshape(256, 128), weights[3 + a].reshape(256, 128)], axis=1
        )
        lat = lat + lax.dot_general(
            hs[2 - a : 6 - a].reshape(256, 256), both, over_last, preferred_element_type=F32
        )
    lat = lat.reshape(4, 4, 16, 256)
    for i in range(2):
        for core in range(2):
            lat_out[i, core] = lat[2 * i : 2 * i + 2, 2 * core : 2 * core + 2]
    out_own[...] = lat_out[s, c]
    for i, (dz, side, core) in enumerate(((0, s, other), (partner, 1 - s, c), (partner, 1 - s, other))):
        send(
            lat_out.at[side, core],
            out_other.at[i],
            lat_sem.at[i],
            lat_sem.at[3 + i],
            dev(u, core, dz),
        )

    kept = {}

    def axis_a(i):
        first, n = chunks[i]
        part = pl.ds(first, n)
        for j in range(1, 4):
            arrived(got_b.at[part, j - 1], rb_recv.at[3 * i + j - 1])
        for k in far_first + (0,):
            at = (pa + k) % 4
            rows = dw[part, pb, at].astype(F32)
            for j in range(3):
                rows = rows + got_b[part, j, at].astype(F32)
            part_b[part, k] = rows.astype(BF16)
            if k:
                sem = 3 * i + k - 1
                send(
                    part_b.at[part, k],
                    got_a.at[part, k - 1],
                    ra_send.at[sem],
                    ra_recv.at[sem],
                    dev(unit(k, 0), c),
                )

    def swap(i):
        first, n = chunks[i]
        part = pl.ds(first, n)
        rows = part_b[part, 0].astype(F32)
        for j in range(1, 4):
            arrived(got_a.at[part, j - 1], ra_recv.at[3 * i + j - 1])
            rows = rows + got_a[part, j - 1].astype(F32)
        swap_out[part] = jnp.where(c == 0, rows[:, 8:16], rows[:, 0:8])
        kept[i] = jnp.where(c == 0, rows[:, 0:8], rows[:, 8:16])
        send(swap_out.at[part], swap_in.at[part], swap_sem.at[i], swap_sem.at[3 + i], sibling)

    mine_at = z // 2

    def z_block(p, slot):
        owner = (p - APART * slot) % 8
        return remote(
            zsend_buf.at[p],
            zrecv_buf.at[slot, mine_at],
            z_send.at[OWNERS * p + slot],
            z_recv.at[8 * slot + mine_at],
            (2 * owner + s, h),
        )

    def along_z(i):
        first, n = chunks[i]
        part = pl.ds(first, n)
        arrived(swap_in.at[part], swap_sem.at[3 + i])
        theirs = swap_in[part]
        zsend_buf[part] = jnp.concatenate(
            [jnp.where(c == 0, kept[i], theirs), jnp.where(c == 0, theirs, kept[i])], axis=1
        ).astype(BF16)
        for p in range(first, first + n):

            for slot in range(OWNERS):

                @pl.when(mine_at != (p - APART * slot) % 8)
                def _():
                    z_block(p, slot).start()

    axis_a(0)
    axis_a(1)
    swap(0)
    axis_a(2)
    token_in(2)
    along_z(0)
    swap(1)
    along_z(1)
    swap(2)
    along_z(2)

    def g_copy(slot, step):
        block = 2 * ((mine_at + APART * slot) % 8) + s
        n = (2 * APART - 1) * slot + (step + APART if step < 0 else step + APART - 1)
        return remote(
            gsend_buf.at[slot], grecv_buf.at[block], g_send.at[n], g_recv.at[block], ((z + step + Z) % Z, h)
        )

    steps = [v for d in range(APART, 0, -1) for v in (-d, d - 1) if v]

    for j in range(OWNERS):
        slot = (j - mine_at // APART + OWNERS) % OWNERS
        block = mine_at % APART + APART * j

        @pl.when(block < BLOCKS)
        def _():
            zrecv_buf[slot, mine_at] = zsend_buf[block]
            for i in (1, 7, 2, 6, 3, 5, 4):
                source = (mine_at + i) % 8
                arrived(zrecv_buf.at[slot, source], z_recv.at[8 * slot + source])
            acc = zrecv_buf[slot, 0].astype(F32)
            for i in range(1, 8):
                acc = acc + zrecv_buf[slot, i].astype(F32)
            gsend_buf[slot] = acc.astype(BF16)
            for step in steps:
                g_copy(slot, step).start()
            grecv_buf[2 * block + s] = gsend_buf[slot]

    for i in range(3):
        arrived(out_other.at[i], lat_sem.at[3 + i])
    for copy in sent:
        copy.wait_send()
    @pl.when(s == 0)
    def _():
        for copy in late_copies():
            copy.wait_send()

    for p in range(BLOCKS):

        for slot in range(OWNERS):

            @pl.when(mine_at != (p - APART * slot) % 8)
            def _():
                z_block(p, slot).wait_send()

    for slot in range(OWNERS):

        @pl.when((mine_at + APART * slot) % 8 < BLOCKS)
        def _():
            for step in steps:
                g_copy(slot, step).wait_send()

    def grad_tap(t, pieces, group):
        out_grad[:, t * 128 : (t + 1) * 128] = SCALE * by_group(
            [turn(pieces[q], q - group) for q in range(4)]
        )

    for p in range(BLOCKS):
        pieces = []
        for i in range(2):
            at = 2 * p + i

            @pl.when((z - at + Z) % (2 * APART) != 0)
            def _():
                arrived(grecv_buf.at[at], g_recv.at[at])

            both = grecv_buf[at].astype(F32)
            pieces += [both[0:8], both[8:16]]
        for g in range(4):
            if p < 6:
                grad_tap(9 * (2 - p // 2) + 4 * (p % 2) + g, pieces, g)
            elif g < 3:
                grad_tap(9 * g + 8, pieces, g)
    whole = (pieces[0] + pieces[1] + pieces[2] + pieces[3])[0:1]
    whole = jnp.where(group_of((1, 128)) == 3, whole, 0.0)
    out_loss[0, 0] = jnp.sum(whole) * (1.0 / 16777216)


def per_device(latent, target_frames, master, first_moment, second_moment, ema_weights):
    vmem = pl.BlockSpec(memory_space=pltpu.VMEM)
    hbm = pl.BlockSpec(memory_space=pltpu.HBM)
    dma = pltpu.SemaphoreType.DMA
    quarter_grad = jax.ShapeDtypeStruct(latent.shape, F32)
    grad, own, other, loss = pl.pallas_call(
        kernel,
        out_shape=(
            jax.ShapeDtypeStruct(master.shape, F32),
            quarter_grad,
            jax.ShapeDtypeStruct((3, *latent.shape), F32),
            jax.ShapeDtypeStruct((1, 1), F32),
        ),
        in_specs=[hbm, hbm, hbm],
        out_specs=(vmem, vmem, vmem, pl.BlockSpec(memory_space=pltpu.SMEM)),
        scratch_shapes=[
            pltpu.VMEM((8, 3456), F32),
            pltpu.VMEM((BLOCKS, 8, 128), F32),
            pltpu.VMEM((BLOCKS, 8, 128), F32),
            pltpu.VMEM((BLOCKS, 16, 16, 128), BF16),
            pltpu.VMEM((8, 6, 16, 256), BF16),
            pltpu.VMEM((6, 6, 16, 768), BF16),
            pltpu.VMEM((2, 4, 32, 128), BF16),
            pltpu.VMEM((256, 128), F32),
            pltpu.VMEM((4, 2, 2, 16, 128), BF16),
            pltpu.VMEM((4, 16, 128), BF16),
            pltpu.VMEM((3, 2, 2, 2, 16, 128), BF16),
            pltpu.VMEM((3, 2, 2, 16, 128), BF16),
            pltpu.VMEM((6, 2, 2, 80, 128), F32),
            pltpu.VMEM((6, 96, 384), F32),
            pltpu.VMEM((6, 64, 256), BF16),
            pltpu.VMEM((6, 64, 128), F32),
            pltpu.VMEM((BLOCKS, 4, 4, 16, 128), BF16),
            pltpu.VMEM((BLOCKS, 3, 4, 16, 128), BF16),
            pltpu.VMEM((BLOCKS, 4, 16, 128), BF16),
            pltpu.VMEM((BLOCKS, 3, 16, 128), BF16),
            pltpu.VMEM((BLOCKS, 8, 128), F32),
            pltpu.VMEM((BLOCKS, 8, 128), F32),
            pltpu.VMEM((BLOCKS, 16, 128), BF16),
            pltpu.VMEM((OWNERS, 8, 16, 128), BF16),
            pltpu.VMEM((OWNERS, 16, 128), BF16),
            pltpu.VMEM((16, 16, 128), BF16),
            pltpu.VMEM((2, 2, 2, 2, 16, 256), F32),
            dma((2,)),
            dma((15,)),
            dma((15,)),
            dma((15,)),
            dma((16,)),
            dma((14,)),
            dma((12,)),
            dma((9,)),
            dma((9,)),
            dma((9,)),
            dma((9,)),
            dma((6,)),
            dma((OWNERS * BLOCKS,)),
            dma((OWNERS * 8,)),
            dma((16,)),
            dma((16,)),
            dma((6,)),
            dma((3,)),
            pltpu.SemaphoreType.REGULAR((3,)),
        ],
        compiler_params=pltpu.CompilerParams(
            collective_id=0, has_side_effects=True, vmem_limit_bytes=40 * 1024 * 1024
        ),
    )(*(pltpu.with_memory_space_constraint(v, pltpu.HBM) for v in (latent, target_frames, master)))
    new_first = beta_first * first_moment + (1.0 - beta_first) * grad
    new_second = beta_second * second_moment + (1.0 - beta_second) * grad * grad
    new_master = master - learn_rate * new_first / (jnp.sqrt(new_second) + adam_eps)
    new_ema = ema_decay * ema_weights + (1.0 - ema_decay) * new_master
    latent_grad = (own + other[0] + other[1] + other[2]).astype(BF16)
    return (new_master, new_first, new_second, new_ema, latent_grad, loss.reshape(()))


def solution(mesh):
    placed = (
        P("tm", "height", None, None),
        P("tm", "height", None, None),
        P("height", None),
        P("height", None),
        P("height", None),
        P("height", None),
    )
    return jax.shard_map(
        per_device,
        mesh=mesh,
        in_specs=placed,
        out_specs=(
            P("height", None),
            P("height", None),
            P("height", None),
            P("height", None),
            P("tm", "height", None, None),
            P(),
        ),
        check_vma=False,
    )
```
